32 devices in a mesh: segment: 2 (over core), ctx: 8 (over z, x), tp: 2 (over y).
Axes of the slice: x: 2, y: 2, z: 4, core: 2. Of those that a mesh axis runs over, the one named last changes fastest.
Arguments:
- queries: bfloat16 [1024, 32, 128], P('ctx', 'tp'), may hold values from -14 to 14
- keys: bfloat16 [1024, 8, 128], P('ctx', 'tp'), may hold values from -10 to 10
- values: bfloat16 [1024, 8, 128], P('ctx', 'tp'), may hold values from -6 to 6
- layer_in: bfloat16 [1024, 4096], P('ctx', 'tp'), may hold values from -6 to 6
- w_bc: bfloat16 [1, 4096, 1024], P(None, 'tp'), may hold values from -0.09375 to 0.09375
- w_dt: bfloat16 [1, 4096, 64], P(None, 'tp'), may hold values from -0.09375 to 0.09375
- dt_bias: float32 [1, 64], P(None, 'tp'), may hold values from -1 to 1
- decay_rate: float32 [1, 64], P(None, 'tp'), may hold values from 9.765625e-05 to 0.06
- skip_gain: float32 [1, 64], P(None, 'tp'), may hold values from 0.5 to 2
- out_gain: float32 [1, 64, 64], P(None, 'tp'), may hold values from 0.5 to 1.5
Outputs:
- section_out: bfloat16 [2, 1024, 4096], P('segment', 'ctx', 'tp')
The draws below stay inside these ranges and needn't reach their ends.
All inputs are finite; a program needn't handle non-finite values.
Results may differ from the reference program's by a relative error of at most 0.002.
Values may be sent and summed in bfloat16 or wider, within the bound.
A program may use at most 256 MiB of HBM per device.

```python
import math
import jax
import jax.numpy as jnp
from jax import lax

QHEADS = 32
KVHEADS = 8
HEAD = 128
SHEADS = 64
SHEAD = 64
GROUPS = 4
STATE = 128
LAYERS = 1
L_DEV = 128
SEQ = 1024


def draw_queries(key, part):
    shape_all = (SEQ, QHEADS, HEAD)
    return jnp.clip(1.7 * jax.random.normal(jax.random.fold_in(key, 1), shape_all, jnp.float32), -10.0, 10.0).astype(jnp.bfloat16)


def draw_keys(key, part):
    shape_all = (SEQ, KVHEADS, HEAD)
    return jnp.clip(1.7 * jax.random.normal(jax.random.fold_in(key, 2), shape_all, jnp.float32), -10.0, 10.0).astype(jnp.bfloat16)


def draw_decay_rate(key, part):
    shape_all = (LAYERS, SHEADS)
    pick_draw = jax.random.uniform(jax.random.fold_in(key, 1), shape_all, jnp.float32)
    slow_rate = jnp.exp(jax.random.uniform(jax.random.fold_in(key, 2), shape_all, jnp.float32, jnp.log(0.1), 0.0)) / SEQ
    fast_rate = jnp.exp(jax.random.uniform(jax.random.fold_in(key, 3), shape_all, jnp.float32, jnp.log(0.02), jnp.log(0.06)))
    slow_share = 0.5
    return jnp.where(pick_draw < slow_share, slow_rate, fast_rate)


def block_scale(rng, extent, shards, least, top_value):
    gain = 1.0
    for axis_at, shards_of in shards:
        steps = jax.random.uniform(jax.random.fold_in(jax.random.fold_in(rng, 6), axis_at), (shards_of,), jnp.float32, least / len(shards), top_value / len(shards))
        gain = gain * jnp.repeat(jnp.exp(steps), extent[axis_at] // shards_of).reshape((-1,) + (1,) * (len(extent) - 1 - axis_at))
    return gain


def normal_values(own_key, shape, scale, most, split=(), kind=jnp.bfloat16):
    values = jax.random.normal(own_key, shape, jnp.float32) * scale
    if len(split) > 0:
        values = block_scale(own_key, shape, split, -0.22, 0.18) * values
    return jnp.clip(values, min=-most, max=most).astype(kind)


def setup_inputs(seed: int = 0) -> dict:
    seeds = jax.random.split(jax.random.key(seed), 11)
    queries = draw_queries(jax.random.fold_in(seeds[10], 71), 0)
    keys = draw_keys(jax.random.fold_in(seeds[10], 71), 0)
    values = normal_values(seeds[2], (SEQ, KVHEADS, HEAD), 1.0, 6.0, ((0, 8), (1, 2)))
    layer_in = normal_values(seeds[3], (SEQ, SHEADS * SHEAD), 1.0, 6.0, ((0, 8), (1, 2)))
    w_bc = normal_values(seeds[4], (LAYERS, SHEADS * SHEAD, 2 * GROUPS * STATE), (SHEADS * SHEAD) ** -0.5, 0.09375, ((1, 2),))
    w_dt = normal_values(seeds[5], (LAYERS, SHEADS * SHEAD, SHEADS), (SHEADS * SHEAD) ** -0.5, 0.09375, ((1, 2),))
    dt_bias = jnp.clip(jax.random.uniform(seeds[6], (LAYERS, SHEADS), jnp.float32, -1.0, 1.0) * block_scale(seeds[6], (LAYERS, SHEADS), ((1, 2),), -0.4, 0.0), -1.0, 1.0)
    decay_rate = draw_decay_rate(jax.random.fold_in(seeds[10], 71), 0)
    skip_gain = jnp.clip(0.5 + 1.5 * jax.random.uniform(seeds[8], (LAYERS, SHEADS), jnp.float32) ** block_scale(seeds[8], (LAYERS, SHEADS), ((1, 2),), -0.2, 0.2), 0.5, 2.0)
    out_gain = jnp.clip(1.0 + 0.1 * jax.random.normal(seeds[9], (LAYERS, SHEADS, SHEAD), jnp.float32), 0.5, 1.5)
    return dict(queries=queries, keys=keys, values=values, layer_in=layer_in, w_bc=w_bc, w_dt=w_dt, dt_bias=dt_bias, decay_rate=decay_rate, skip_gain=skip_gain, out_gain=out_gain)


EPSILON = 1e-05

def span_terms(normed, b_rows, c_rows, step_sizes, rate_row, skip_row):
    count_rows, head_count, head_width = normed.shape
    group_count = b_rows.shape[1]
    per_group = head_count // group_count
    state_root = math.sqrt(b_rows.shape[2])
    log_decay = jnp.cumsum(-step_sizes * rate_row[None, :], axis=0)
    lower_mask = jnp.arange(count_rows)[:, None] >= jnp.arange(count_rows)[None, :]
    intersection = jnp.einsum('tgn,sgn->gts', c_rows, b_rows, precision=lax.Precision.HIGHEST) / state_root
    log_gaps = log_decay.T[:, :, None] - log_decay.T[:, None, :]
    decays = jnp.where(lower_mask[None], jnp.exp(jnp.where(lower_mask[None], log_gaps, 0.0)), 0.0)
    mixing = decays.reshape(group_count, per_group, count_rows, count_rows) * intersection[:, None] * step_sizes.T.reshape(group_count, per_group, 1, count_rows)
    grouped = normed.reshape(count_rows, group_count, per_group, head_width)
    local_part = jnp.einsum('gkts,sgkp->tgkp', mixing, grouped, precision=lax.Precision.HIGHEST).reshape(count_rows, head_count, head_width)
    tail_weight = jnp.exp(log_decay[-1][None, :] - log_decay) * step_sizes
    weighted = (normed * tail_weight[:, :, None]).reshape(count_rows, group_count, per_group, head_width)
    ending = jnp.einsum('sgkp,sgn->gkpn', weighted, b_rows, precision=lax.Precision.HIGHEST).reshape(head_count, head_width, b_rows.shape[2])
    return (log_decay, local_part + skip_row[None, :, None] * normed, ending, jnp.exp(log_decay[-1]))

def span_inflow(log_decay, c_rows, state_in):
    count_rows, group_count, state_n = c_rows.shape
    head_count, head_width = (state_in.shape[0], state_in.shape[1])
    per_group = head_count // group_count
    state_root = math.sqrt(state_n)
    inflow = jnp.einsum('tgn,gkpn->tgkp', c_rows, state_in.reshape(group_count, per_group, head_width, state_n), precision=lax.Precision.HIGHEST)
    return jnp.exp(log_decay)[:, :, None] * inflow.reshape(count_rows, head_count, head_width) / state_root

def attend_one(queries, keys, values):
    group_size = queries.shape[1] // keys.shape[1]
    score_scale = 1.0 / math.sqrt(queries.shape[2])
    positions = jnp.arange(queries.shape[0])
    causal = positions[:, None] >= positions[None, :]

    def one_head(head_index):
        q_one = lax.dynamic_index_in_dim(queries, head_index, 1, keepdims=False)
        k_one = lax.dynamic_index_in_dim(keys, head_index // group_size, 1, keepdims=False)
        v_one = lax.dynamic_index_in_dim(values, head_index // group_size, 1, keepdims=False)
        scores = jnp.dot(q_one, k_one.T, preferred_element_type=jnp.float32) * score_scale
        scores = jnp.where(causal, scores, -jnp.inf)
        row_top = lax.optimization_barrier(jnp.max(scores, axis=1, keepdims=True))
        raw_weight = jnp.exp(scores - row_top)
        row_total = lax.optimization_barrier(jnp.sum(raw_weight, axis=1, keepdims=True))
        mixed_out = jnp.dot(raw_weight.astype(jnp.bfloat16), v_one, preferred_element_type=jnp.float32) / row_total
        return mixed_out.astype(jnp.bfloat16)
    heads_out = lax.map(one_head, jnp.arange(queries.shape[1], dtype=jnp.int32))
    return heads_out.transpose(1, 0, 2).reshape(queries.shape[0], queries.shape[1] * queries.shape[2])

def state_layer(inputs, w_bc, w_dt, dt_bias, decay_rate, skip_gain, out_gain):
    seq_len, channel_count = inputs.shape
    head_count = decay_rate.shape[0]
    head_width = channel_count // head_count
    proj_bc = jnp.dot(inputs, w_bc, preferred_element_type=jnp.float32)
    proj_dt = jnp.dot(inputs, w_dt, preferred_element_type=jnp.float32)
    wide_rows = inputs.astype(jnp.float32)
    inv_rms = lax.rsqrt(lax.optimization_barrier(jnp.sum(wide_rows * wide_rows, axis=1)) / channel_count + EPSILON)
    normed = (wide_rows * inv_rms[:, None]).reshape(seq_len, head_count, head_width)
    half_cols = w_bc.shape[1] // 2
    b_rows = (proj_bc[:, :half_cols] * inv_rms[:, None]).reshape(seq_len, GROUPS, STATE)
    c_rows = (proj_bc[:, half_cols:] * inv_rms[:, None]).reshape(seq_len, GROUPS, STATE)
    step_sizes = jax.nn.softplus(proj_dt * inv_rms[:, None] + dt_bias[None, :])
    block_count = seq_len // L_DEV

    def split_rows(array):
        return array.reshape((block_count, L_DEV) + array.shape[1:])

    def one_block(carried, pieces):
        normed_b, b_b, c_b, step_b = pieces
        log_decay, local_part, ending, span_decay = span_terms(normed_b, b_b, c_b, step_b, decay_rate, skip_gain)
        mixed_out = local_part + span_inflow(log_decay, c_b, carried)
        return (span_decay[:, None, None] * carried + ending, mixed_out)
    initial = jnp.zeros((head_count, head_width, STATE), jnp.float32)
    _, mixed_blocks = lax.scan(one_block, initial, (split_rows(normed), split_rows(b_rows), split_rows(c_rows), split_rows(step_sizes)))
    mixed_out = mixed_blocks.reshape(seq_len, head_count, head_width)
    power = lax.optimization_barrier(jnp.mean(mixed_out * mixed_out, axis=2, keepdims=True))
    result = wide_rows.reshape(seq_len, head_count, head_width) + out_gain[None] * mixed_out * lax.rsqrt(power + EPSILON)
    return result.reshape(seq_len, channel_count).astype(jnp.bfloat16)

def reference(queries, keys, values, layer_in, w_bc, w_dt, dt_bias, decay_rate, skip_gain, out_gain):
    attended = attend_one(queries, keys, values)
    current = layer_in
    for layer_index in range(LAYERS):
        current = state_layer(current, w_bc[layer_index], w_dt[layer_index], dt_bias[layer_index], decay_rate[layer_index], skip_gain[layer_index], out_gain[layer_index])
    return jnp.stack([current, attended])
```

```python
import functools
import math

import jax
import jax.numpy as jnp
from jax import lax
from jax.experimental import pallas as pl
from jax.experimental.pallas import tpu as pltpu
from jax.sharding import PartitionSpec as P

MESH = pl.DeviceIdType.MESH
EPSILON = 1e-05
F32 = jnp.float32
BF16 = jnp.bfloat16

ROWS = 128
HEAD = 128
STATE = 128
SHEAD = 64
GHEADS = 16
GCOLS = GHEADS * SHEAD
GROUPS = 4
QH = 8
CHUNKS = 4
CCOLS = GCOLS // CHUNKS
MISC = 24
PACK = 2 * ROWS + MISC


def split(a):
    hi = a.astype(BF16)
    return hi, (a - hi.astype(F32)).astype(BF16)


def dot(a, b):
    return jnp.dot(a, b, preferred_element_type=F32)


def dot_t(a, b):
    return lax.dot_general(a, b, (((1,), (1,)), ((), ())), preferred_element_type=F32)


def dot3(a, b):
    return dot(a[0], b[0]) + (dot(a[0], b[1]) + dot(a[1], b[0]))


def dot3_t(a, b):
    return dot_t(a[0], b[0]) + (dot_t(a[0], b[1]) + dot_t(a[1], b[0]))


def lane_pair(left, right, shape):
    lane = lax.broadcasted_iota(jnp.int32, shape, 1)
    return jnp.where(lane < SHEAD, jnp.broadcast_to(left, shape), jnp.broadcast_to(right, shape))


def kernel(
    nz,
    q_hbm,
    kv_hbm,
    x_hbm,
    w_hbm,
    wdt_hbm,
    par_ref,
    row_ref,
    out_ref,
    qbuf,
    kvbuf,
    scores,
    xv,
    wv,
    wdtv,
    xg,
    psend,
    pbuf,
    tcols,
    rows_s,
    bt_s,
    c_s,
    cb_s,
    ending,
    s_in,
    s_out,
    local,
    stage,
    loc_sem,
    q_sem,
    kv_send,
    kv_recv,
    x_sem,
    p_send,
    p_recv,
    st_send,
    st_recv,
    o_send,
    o_recv,
):
    seg = lax.axis_index("segment")
    ctx = lax.axis_index("ctx")
    tp = lax.axis_index("tp")
    z = ctx // 2
    half = ctx % 2
    other = 1 - half
    pair = z * 2 + other
    barrier = pltpu.get_barrier_semaphore()
    my_rows = pl.ds(pl.multiple_of(half * ROWS, ROWS), ROWS)
    other_rows = pl.ds(pl.multiple_of(other * ROWS, ROWS), ROWS)
    my_cols = pl.ds(pl.multiple_of(half * GCOLS, GCOLS), GCOLS)
    other_cols = pl.ds(pl.multiple_of(other * GCOLS, GCOLS), GCOLS)

    def signal(s, c, t):
        pl.semaphore_signal(barrier, inc=1, device_id=(s, c, t), device_id_type=MESH)

    def remote(src, dst, send, recv, c, t):
        return pltpu.make_async_remote_copy(
            src_ref=src,
            dst_ref=dst,
            send_sem=send,
            recv_sem=recv,
            device_id=(seg, c, t),
            device_id_type=MESH,
        )

    @pl.when(seg == 1)
    def _attention():
        own_q = pltpu.make_async_copy(q_hbm.at[half], qbuf.at[:, my_rows, :], loc_sem.at[0])
        own_kv = pltpu.make_async_copy(kv_hbm.at[half], kvbuf.at[z, :, my_rows, :], loc_sem.at[1])
        own_q.start()
        own_kv.start()
        signal(1, pair, tp)

        def greet(zz, carry):
            signal(1, zz * 2, tp)
            signal(1, zz * 2 + 1, tp)
            return carry

        lax.fori_loop(0, z, greet, 0)
        pl.semaphore_wait(barrier, 1 + 2 * (nz - 1 - z))

        def kv_copy(part, c):
            return remote(
                kv_hbm.at[part], kvbuf.at[z, :, my_rows, :], kv_send.at[c], kv_recv.at[ctx], c, tp
            )

        def kv_arrival(c, src_z, src_rows):
            return remote(
                kv_hbm.at[half], kvbuf.at[src_z, :, src_rows, :], kv_send.at[c], kv_recv.at[c], c, tp
            )

        def q_copy(dst_rows):
            return remote(
                q_hbm.at[other], qbuf.at[:, dst_rows, :], q_sem.at[0], q_sem.at[1], pair, tp
            )

        def start_far(zz, carry):
            kv_copy(0, zz * 2).start()
            kv_copy(1, zz * 2 + 1).start()
            return carry

        lax.fori_loop(z + 1, nz, start_far, 0)
        kv_copy(other, pair).start()
        q_copy(my_rows).start()
        own_q.wait()
        own_kv.wait()
        q_copy(other_rows).wait_recv()
        kv_arrival(pair, z, other_rows).wait_recv()

        def arrive(zz, carry):
            kv_arrival(zz * 2, zz, pl.ds(0, ROWS)).wait_recv()
            kv_arrival(zz * 2 + 1, zz, pl.ds(ROWS, ROWS)).wait_recv()
            return carry

        lax.fori_loop(0, z, arrive, 0)
        scale = 1.0 / math.sqrt(HEAD)
        span = 2 * ROWS
        rows2 = 2 * span
        t_at = lax.broadcasted_iota(jnp.int32, (rows2, span), 0) % span
        s_at = lax.broadcasted_iota(jnp.int32, (rows2, span), 1)
        allowed = t_at >= s_at

        def two_heads(i, carry):
            kvh = i // 2
            q = qbuf[pl.ds(i * 2, 2)].reshape(rows2, HEAD)
            diag = dot_t(q, kvbuf[z, kvh]) * scale
            diag = jnp.where(allowed, diag, -1e30)

            def first(zz, top):
                s = dot_t(q, kvbuf[zz, kvh]) * scale
                scores[zz] = s
                return jnp.maximum(top, jnp.max(s, axis=1, keepdims=True))

            top = lax.fori_loop(0, z, first, jnp.max(diag, axis=1, keepdims=True))
            weight = jnp.exp(diag - top)
            total = jnp.sum(weight, axis=1, keepdims=True)
            acc = dot(weight.astype(BF16), kvbuf[z, kvh + 2])

            def second(zz, kept):
                total, acc = kept
                weight = jnp.exp(scores[zz] - top)
                return (
                    total + jnp.sum(weight, axis=1, keepdims=True),
                    acc + dot(weight.astype(BF16), kvbuf[zz, kvh + 2]),
                )

            total, acc = lax.fori_loop(0, z, second, (total, acc))
            done = (acc / total).astype(BF16)
            for k in range(2):
                cols = pl.ds(pl.multiple_of((i * 2 + k) * HEAD, HEAD), HEAD)
                stage[:, cols] = done[k * span : (k + 1) * span]
            return carry

        lax.fori_loop(0, QH // 2, two_heads, 0)

        def out_copy(cols):
            return remote(
                stage.at[other_rows, :], out_ref.at[:, cols], o_send.at[0], o_recv.at[0], pair, tp
            )

        out_copy(my_cols).start()
        out_ref[:, my_cols] = stage[my_rows, :]
        out_copy(my_cols).wait_send()
        out_copy(other_cols).wait_recv()

        def sent(zz, carry):
            kv_copy(0, zz * 2).wait_send()
            kv_copy(1, zz * 2 + 1).wait_send()
            return carry

        lax.fori_loop(z + 1, nz, sent, 0)
        kv_copy(other, pair).wait_send()
        q_copy(my_rows).wait_send()

    @pl.when(seg == 0)
    def _state():
        me4 = tp * 2 + half
        get_w = pltpu.make_async_copy(w_hbm, wv, loc_sem.at[0])
        get_x = pltpu.make_async_copy(x_hbm, xv, loc_sem.at[1])
        get_dt = pltpu.make_async_copy(wdt_hbm, wdtv, loc_sem.at[2])
        get_g = pltpu.make_async_copy(x_hbm.at[:, my_cols], xg.at[my_rows, :], loc_sem.at[3])
        get_x.start()
        get_w.start()
        get_dt.start()
        get_g.start()
        quad = ((z * 2 + half, 1 - tp), (pair, 1 - tp), (pair, tp))
        for c, t in quad:
            signal(0, c, t)

        @pl.when(z > 0)
        def _():
            signal(0, ctx - 2, tp)

        more = jnp.where(z < nz - 1, 1, 0)
        pl.semaphore_wait(barrier, 3 + more)

        def x_copy(dst_rows):
            return remote(
                x_hbm.at[:, other_cols], xg.at[dst_rows, :], x_sem.at[0], x_sem.at[1], pair, tp
            )

        x_copy(my_rows).start()
        get_x.wait()
        get_dt.wait()
        get_w.wait()
        x = xv[...]
        proj = dot(x, wv[...])
        dt_all = lax.dot_general(
            wdtv[...], x, (((0,), (1,)), ((), ())), preferred_element_type=F32
        )
        wide = x.astype(F32)
        sq_col = jnp.sum(wide * wide, axis=1, keepdims=True)
        sq_row = jnp.transpose(jnp.broadcast_to(sq_col, (ROWS, ROWS)))[0:8]
        for g in range(GROUPS):
            psend[g, 0:ROWS] = proj[:, g * STATE : (g + 1) * STATE]
            psend[g, ROWS : 2 * ROWS] = proj[:, (GROUPS + g) * STATE : (GROUPS + g + 1) * STATE]
            psend[g, 2 * ROWS : 2 * ROWS + GHEADS] = dt_all[g * GHEADS : (g + 1) * GHEADS]
            psend[g, 2 * ROWS + GHEADS : PACK] = sq_row

        def p_copy(k, slot):
            c, t = quad[k]
            to4 = t * 2 + c % 2
            return remote(
                psend.at[to4], pbuf.at[slot], p_send.at[k], p_recv.at[k], c, t
            )

        for k in range(3):
            p_copy(k, me4).start()
        pbuf[me4] = psend[me4]
        get_g.wait()
        x_copy(other_rows).wait_recv()
        for k in range(3):
            c, t = quad[k]
            p_copy(k, t * 2 + c % 2).wait_recv()

        span = 2 * ROWS
        r0 = pbuf[0] + pbuf[2]
        r1 = pbuf[1] + pbuf[3]
        b = jnp.concatenate([r0[0:ROWS], r1[0:ROWS]], axis=0)
        c_raw = jnp.concatenate([r0[ROWS : 2 * ROWS], r1[ROWS : 2 * ROWS]], axis=0)
        misc = jnp.concatenate([r0[2 * ROWS :], r1[2 * ROWS :]], axis=1)
        channels = 4 * GCOLS
        inv8 = lax.rsqrt(misc[GHEADS:MISC] / channels + EPSILON)
        inv = inv8[0:1]
        heads = pl.ds(pl.multiple_of(half * GHEADS, GHEADS), GHEADS)
        bias = par_ref[0, heads]
        rate = par_ref[1, heads]
        pre = misc[0:GHEADS] * inv + bias
        step = jnp.maximum(pre, 0.0) + jnp.log1p(jnp.exp(-jnp.abs(pre)))
        neg = -(step * rate)
        upto = (
            lax.broadcasted_iota(jnp.int32, (span, span), 0)
            <= lax.broadcasted_iota(jnp.int32, (span, span), 1)
        ).astype(F32).astype(BF16)
        n0 = neg.astype(BF16)
        rest = neg - n0.astype(F32)
        n1 = rest.astype(BF16)
        n2 = (rest - n1.astype(F32)).astype(BF16)
        log_decay = dot(n0, upto) + (dot(n1, upto) + dot(n2, upto))
        log_end = log_decay[:, span - 1 : span]
        u = step * inv
        root = math.sqrt(STATE)
        tall = jnp.concatenate(
            [
                log_decay,
                jnp.exp(log_end - log_decay) * u * inv,
                jnp.exp(log_decay) * inv / root,
                inv8,
                jnp.zeros((STATE - 3 * GHEADS - 8, span), F32),
            ],
            axis=0,
        )
        cols = jnp.transpose(tall)
        tcols[...] = cols
        rows_s[0] = log_decay
        rows_s[1] = u
        inv_col = cols[:, 3 * GHEADS : 3 * GHEADS + 1]
        bt_hi, bt_lo = split(jnp.transpose(b))
        c_hi, c_lo = split(c_raw)
        c_s[0] = c_hi
        c_s[1] = c_lo
        cb = dot3((c_hi, c_lo), (bt_hi, bt_lo)) * inv_col * inv / root
        lower = (
            lax.broadcasted_iota(jnp.int32, (span, span), 0)
            >= lax.broadcasted_iota(jnp.int32, (span, span), 1)
        )
        cb_s[...] = jnp.where(lower, cb, 0.0)

        def columns(base, j):
            parts = []
            for k in range(2):
                h = base + 4 * j + 2 * k
                parts.append(
                    lane_pair(cols[:, h : h + 1], cols[:, h + 1 : h + 2], (span, 2 * SHEAD))
                )
            return jnp.concatenate(parts, axis=1)

        def state_copy(j):
            return remote(
                s_out.at[j], s_in.at[j], st_send.at[j], st_recv.at[j],
                lax.rem(ctx + 2, 2 * nz), tp,
            )

        for j in range(CHUNKS):
            xc = xg[:, j * CCOLS : (j + 1) * CCOLS].astype(F32)
            e = dot3((bt_hi, bt_lo), split(xc * columns(GHEADS, j)))
            ending[j] = e

            @pl.when(z == 0)
            def _():
                s_out[j] = e
                s_in[j] = jnp.zeros_like(e)
                state_copy(j).start()

        for j in range(CHUNKS):
            for k in range(2):
                h = 4 * j + 2 * k
                xp = xg[:, h * SHEAD : (h + 2) * SHEAD]
                halves = []
                for d in range(2):
                    lrow = rows_s[0, h + d : h + d + 1]
                    urow = rows_s[1, h + d : h + d + 1]
                    lcol = tcols[:, h + d : h + d + 1]
                    top = (
                        jnp.exp(jnp.minimum(lcol[:ROWS] - lrow[:, :ROWS], 0.0))
                        * cb_s[:ROWS, :ROWS]
                        * urow[:, :ROWS]
                    )
                    low = jnp.exp(jnp.minimum(lcol[ROWS:] - lrow, 0.0)) * cb_s[ROWS:] * urow
                    t_hi, t_lo = split(top)
                    l_hi, l_lo = split(low)
                    halves.append(
                        (
                            dot(t_hi, xp[:ROWS]) + dot(t_lo, xp[:ROWS]),
                            dot(l_hi, xp) + dot(l_lo, xp),
                        )
                    )
                lane = lax.broadcasted_iota(jnp.int32, (ROWS, 2 * SHEAD), 1)
                at = slice(h * SHEAD, (h + 2) * SHEAD)
                local[0:ROWS, at] = jnp.where(lane < SHEAD, halves[0][0], halves[1][0])
                local[ROWS:span, at] = jnp.where(lane < SHEAD, halves[0][1], halves[1][1])

            @pl.when(z > 0)
            def _():
                state_copy(j).wait_recv()

                @pl.when(z < nz - 1)
                def _():
                    fade = []
                    for k in range(2):
                        h = 4 * j + 2 * k
                        last = tcols[span - 8 : span, 0:STATE][7:8]
                        fade.append(
                            lane_pair(
                                jnp.exp(last[:, h : h + 1]),
                                jnp.exp(last[:, h + 1 : h + 2]),
                                (1, 2 * SHEAD),
                            )
                        )
                    s_out[j] = s_in[j] * jnp.concatenate(fade, axis=1) + ending[j]
                    state_copy(j).start()

        block = (
            lax.broadcasted_iota(jnp.int32, (CCOLS, CCOLS), 0) // SHEAD
            == lax.broadcasted_iota(jnp.int32, (CCOLS, CCOLS), 1) // SHEAD
        ).astype(F32).astype(BF16)

        def out_copy(j, base):
            at = pl.ds(pl.multiple_of(base * GCOLS + j * CCOLS, CCOLS), CCOLS)
            return remote(
                stage.at[other_rows, pl.ds(j * CCOLS, CCOLS)],
                out_ref.at[:, at],
                o_send.at[j],
                o_recv.at[j],
                pair,
                tp,
            )

        for j in range(CHUNKS):
            at = slice(j * CCOLS, (j + 1) * CCOLS)
            xc = xg[:, at].astype(F32)
            inflow = dot3((c_s[0], c_s[1]), split(s_in[j]))
            gcols = pl.ds(pl.multiple_of(half * GCOLS + j * CCOLS, CCOLS), CCOLS)
            skip = row_ref[0:1, gcols]
            gain = row_ref[1:2, gcols]
            mixed = local[:, at] + inflow * columns(2 * GHEADS, j) + skip * (xc * inv_col)
            p_hi, p_lo = split(mixed * mixed)
            power = (dot(p_hi, block) + dot(p_lo, block)) / SHEAD
            stage[:, at] = (xc + gain * mixed * lax.rsqrt(power + EPSILON)).astype(BF16)
            out_copy(j, half).start()
            out_ref[:, gcols] = stage[my_rows, at]

        for j in range(CHUNKS):
            out_copy(j, half).wait_send()
            out_copy(j, other).wait_recv()

            @pl.when(z < nz - 1)
            def _():
                state_copy(j).wait_send()

        for k in range(3):
            p_copy(k, me4).wait_send()
        x_copy(my_rows).wait_send()


def body(queries, keys, values, layer_in, w_bc, w_dt, dt_bias, decay_rate, skip_gain, out_gain):
    nctx = lax.axis_size("ctx")
    nz = nctx // 2
    span = 2 * ROWS
    q = queries.transpose(1, 0, 2).reshape(2, QH, ROWS, HEAD)
    kv = jnp.stack([keys.reshape(ROWS, 2, 2, HEAD), values.reshape(ROWS, 2, 2, HEAD)], axis=0)
    kv = kv.transpose(2, 0, 3, 1, 4).reshape(2, 4, ROWS, HEAD)
    heads = dt_bias.shape[1]
    par = jnp.broadcast_to(
        jnp.concatenate([dt_bias, decay_rate], axis=0)[:, :, None], (2, heads, span)
    )
    lane_rows = jnp.concatenate(
        [jnp.repeat(skip_gain, SHEAD, axis=1), out_gain.reshape(1, heads * SHEAD)], axis=0
    )
    any_spec = pl.BlockSpec(memory_space=pl.ANY)
    vmem_spec = pl.BlockSpec(memory_space=pltpu.VMEM)
    dma = pltpu.SemaphoreType.DMA
    vm = pltpu.VMEM
    out = pl.pallas_call(
        functools.partial(kernel, nz),
        out_shape=jax.ShapeDtypeStruct(layer_in.shape, BF16),
        in_specs=[any_spec] * 5 + [vmem_spec] * 2,
        out_specs=vmem_spec,
        scratch_shapes=[
            vm((QH, span, HEAD), BF16),
            vm((nz, 4, span, HEAD), BF16),
            vm((nz, 2 * span, span), F32),
            vm(layer_in.shape, BF16),
            vm(w_bc.shape[1:], BF16),
            vm(w_dt.shape[1:], BF16),
            vm((span, GCOLS), BF16),
            vm((GROUPS, PACK, STATE), F32),
            vm((GROUPS, PACK, STATE), F32),
            vm((span, STATE), F32),
            vm((2, GHEADS, span), F32),
            vm((8, STATE), BF16),
            vm((2, span, STATE), BF16),
            vm((span, span), F32),
            vm((CHUNKS, STATE, CCOLS), F32),
            vm((CHUNKS, STATE, CCOLS), F32),
            vm((CHUNKS, STATE, CCOLS), F32),
            vm((span, GCOLS), F32),
            vm((span, GCOLS), BF16),
            dma((4,)),
            dma((2,)),
            dma((nctx,)),
            dma((nctx,)),
            dma((2,)),
            dma((3,)),
            dma((3,)),
            dma((CHUNKS,)),
            dma((CHUNKS,)),
            dma((CHUNKS,)),
            dma((CHUNKS,)),
        ],
        compiler_params=pltpu.CompilerParams(
            collective_id=0, has_side_effects=True, vmem_limit_bytes=52 * 1024 * 1024
        ),
    )(q, kv, layer_in, w_bc[0], w_dt[0], par, lane_rows)
    return out[None]


def solution(mesh):
    in_specs = (
        P("ctx", "tp", None),
        P("ctx", "tp", None),
        P("ctx", "tp", None),
        P("ctx", "tp"),
        P(None, "tp", None),
        P(None, "tp", None),
        P(None, "tp"),
        P(None, "tp"),
        P(None, "tp"),
        P(None, "tp", None),
    )
    out_specs = P("segment", "ctx", "tp")
    return jax.shard_map(body, mesh=mesh, in_specs=in_specs, out_specs=out_specs, check_vma=False)
```

```python
import functools
import math

import jax
import jax.numpy as jnp
from jax import lax
from jax.experimental import pallas as pl
from jax.experimental.pallas import tpu as pltpu
from jax.sharding import PartitionSpec as P

MESH = pl.DeviceIdType.MESH
EPSILON = 1e-05
F32 = jnp.float32
BF16 = jnp.bfloat16

ROWS = 128
HEAD = 128
STATE = 128
SHEAD = 64
GHEADS = 16
GCOLS = GHEADS * SHEAD
GROUPS = 4
QH = 8
CHUNKS = 8
CCOLS = GCOLS // CHUNKS
MISC = 24
PACK = 2 * ROWS + MISC


def split(a):
    hi = a.astype(BF16)
    return hi, (a - hi.astype(F32)).astype(BF16)


def dot(a, b):
    return jnp.dot(a, b, preferred_element_type=F32)


def dot_t(a, b):
    return lax.dot_general(a, b, (((1,), (1,)), ((), ())), preferred_element_type=F32)


def dot3(a, b):
    return dot(a[0], b[0]) + (dot(a[0], b[1]) + dot(a[1], b[0]))


def dot3_t(a, b):
    return dot_t(a[0], b[0]) + (dot_t(a[0], b[1]) + dot_t(a[1], b[0]))


def lane_pair(left, right, shape):
    lane = lax.broadcasted_iota(jnp.int32, shape, 1)
    return jnp.where(lane < SHEAD, jnp.broadcast_to(left, shape), jnp.broadcast_to(right, shape))


def head_column(ref, half):
    shape = (GHEADS, ref.shape[1])
    wanted = lax.broadcasted_iota(jnp.int32, shape, 1) == (
        lax.broadcasted_iota(jnp.int32, shape, 0) + half * GHEADS
    )
    return jnp.sum(
        jnp.where(wanted, jnp.broadcast_to(ref[...], shape), 0.0), axis=1, keepdims=True
    )


def channel_rows(skip_ref, gain_ref, half):
    shape = (GHEADS, GCOLS)
    own = (
        lax.broadcasted_iota(jnp.int32, shape, 1) // SHEAD
        == lax.broadcasted_iota(jnp.int32, shape, 0)
    )
    skip = jnp.broadcast_to(head_column(skip_ref, half), shape)
    skip = jnp.sum(jnp.where(own, skip, 0.0), axis=0, keepdims=True)
    gain = gain_ref[pl.ds(pl.multiple_of(half * GHEADS, GHEADS), GHEADS), :]
    pairs = jnp.concatenate([gain, gain], axis=1)
    gain = jnp.concatenate([pairs] * (GHEADS // 2), axis=1)
    gain = jnp.sum(jnp.where(own, gain, 0.0), axis=0, keepdims=True)
    return skip, gain


def kernel(
    nz,
    q_hbm,
    k_hbm,
    v_hbm,
    x_hbm,
    w_hbm,
    wdt_hbm,
    bias_ref,
    rate_ref,
    skip_ref,
    gain_ref,
    out_ref,
    q_in,
    k_in,
    v_in,
    q_own,
    kv_own,
    qbuf,
    kvbuf,
    scores,
    xv,
    wv,
    wdtv,
    xg,
    psend,
    psend_dt,
    pbuf,
    tcols,
    rows_s,
    bt_s,
    c_s,
    cb_s,
    ending,
    s_in,
    s_out,
    local,
    stage,
    loc_sem,
    w_sem,
    q_sem,
    pkv_sem,
    kv_send,
    kv_recv,
    x_sem,
    p_send,
    p_recv,
    st_send,
    st_recv,
    o_send,
    o_recv,
):
    seg = lax.axis_index("segment")
    ctx = lax.axis_index("ctx")
    tp = lax.axis_index("tp")
    z = ctx // 2
    half = ctx % 2
    other = 1 - half
    pair = z * 2 + other
    barrier = pltpu.get_barrier_semaphore()
    my_rows = pl.ds(pl.multiple_of(half * ROWS, ROWS), ROWS)
    other_rows = pl.ds(pl.multiple_of(other * ROWS, ROWS), ROWS)
    my_cols = pl.ds(pl.multiple_of(half * GCOLS, GCOLS), GCOLS)
    other_cols = pl.ds(pl.multiple_of(other * GCOLS, GCOLS), GCOLS)

    def signal(s, c, t):
        pl.semaphore_signal(barrier, inc=1, device_id=(s, c, t), device_id_type=MESH)

    def remote(src, dst, send, recv, c, t):
        return pltpu.make_async_remote_copy(
            src_ref=src,
            dst_ref=dst,
            send_sem=send,
            recv_sem=recv,
            device_id=(seg, c, t),
            device_id_type=MESH,
        )

    @pl.when(seg == 1)
    def _attention():
        get_k = pltpu.make_async_copy(k_hbm, k_in, loc_sem.at[0])
        get_v = pltpu.make_async_copy(v_hbm, v_in, loc_sem.at[1])
        get_q = pltpu.make_async_copy(q_hbm, q_in, loc_sem.at[2])
        get_k.start()
        get_v.start()
        get_q.start()
        signal(1, pair, tp)

        @pl.when(z > 0)
        def _():
            signal(1, ctx - 2, tp)

        get_k.wait()
        get_v.wait()
        k_heads = jnp.swapaxes(k_in[...].astype(F32), 0, 1).astype(BF16)
        v_heads = jnp.swapaxes(v_in[...].astype(F32), 0, 1).astype(BF16)
        for p in range(2):
            kv_own[p, 0:2] = k_heads[2 * p : 2 * p + 2]
            kv_own[p, 2:4] = v_heads[2 * p : 2 * p + 2]
        pl.semaphore_wait(barrier, 1 + jnp.where(z < nz - 1, 1, 0))
        following = lax.rem(ctx + 2, 2 * nz)

        def pair_copy(dst_rows):
            return remote(
                kv_own.at[other], kvbuf.at[z, :, dst_rows, :], pkv_sem.at[0], pkv_sem.at[1], pair, tp
            )

        def pass_on(zz):
            return remote(
                kvbuf.at[zz], kvbuf.at[zz], kv_send.at[zz], kv_recv.at[zz], following, tp
            )

        def q_copy(dst_rows):
            return remote(
                q_own.at[other], qbuf.at[:, dst_rows, :], q_sem.at[0], q_sem.at[1], pair, tp
            )

        pair_copy(my_rows).start()
        kvbuf[z, :, my_rows, :] = kv_own[half]
        get_q.wait()
        q_own[...] = (
            jnp.swapaxes(q_in[...].astype(F32), 0, 1).astype(BF16).reshape(2, QH, ROWS, HEAD)
        )
        qbuf[:, my_rows, :] = q_own[half]
        pair_copy(other_rows).wait_recv()

        @pl.when(z < nz - 1)
        def _():
            pass_on(z).start()

        q_copy(my_rows).start()

        def arrive(k, carry):
            zz = z - 1 - k
            pass_on(zz).wait_recv()

            @pl.when(z < nz - 1)
            def _():
                pass_on(zz).start()

            return carry

        lax.fori_loop(0, z, arrive, 0)
        q_copy(other_rows).wait_recv()
        scale = 1.0 / math.sqrt(HEAD)
        span = 2 * ROWS
        rows2 = 2 * span
        t_at = lax.broadcasted_iota(jnp.int32, (rows2, span), 0) % span
        s_at = lax.broadcasted_iota(jnp.int32, (rows2, span), 1)
        allowed = t_at >= s_at

        def two_heads(i, carry):
            kvh = i // 2
            q = qbuf[pl.ds(i * 2, 2)].reshape(rows2, HEAD)
            diag = dot_t(q, kvbuf[z, kvh]) * scale
            diag = jnp.where(allowed, diag, -1e30)

            def first(zz, top):
                s = dot_t(q, kvbuf[zz, kvh]) * scale
                scores[zz] = s
                return jnp.maximum(top, jnp.max(s, axis=1, keepdims=True))

            top = lax.fori_loop(0, z, first, jnp.max(diag, axis=1, keepdims=True))
            weight = jnp.exp(diag - top)
            total = jnp.sum(weight, axis=1, keepdims=True)
            acc = dot(weight.astype(BF16), kvbuf[z, kvh + 2])

            def second(zz, kept):
                total, acc = kept
                weight = jnp.exp(scores[zz] - top)
                return (
                    total + jnp.sum(weight, axis=1, keepdims=True),
                    acc + dot(weight.astype(BF16), kvbuf[zz, kvh + 2]),
                )

            total, acc = lax.fori_loop(0, z, second, (total, acc))
            done = (acc / total).astype(BF16)
            for k in range(2):
                cols = pl.ds(pl.multiple_of((i * 2 + k) * HEAD, HEAD), HEAD)
                stage[:, cols] = done[k * span : (k + 1) * span]
            at = pl.ds(pl.multiple_of(i * 2 * HEAD, 2 * HEAD), 2 * HEAD)
            to = pl.ds(pl.multiple_of(half * GCOLS + i * 2 * HEAD, 2 * HEAD), 2 * HEAD)
            out_copy(i, half).start()
            out_ref[:, to] = stage[my_rows, at]
            return carry

        def out_copy(i, base):
            at = pl.ds(pl.multiple_of(i * 2 * HEAD, 2 * HEAD), 2 * HEAD)
            to = pl.ds(pl.multiple_of(base * GCOLS + i * 2 * HEAD, 2 * HEAD), 2 * HEAD)
            return remote(
                stage.at[other_rows, at], out_ref.at[:, to], o_send.at[i], o_recv.at[i], pair, tp
            )

        lax.fori_loop(0, QH // 2, two_heads, 0)
        for i in range(QH // 2):
            out_copy(i, half).wait_send()
            out_copy(i, other).wait_recv()

        @pl.when(z < nz - 1)
        def _():
            def sent(zz, carry):
                pass_on(zz).wait_send()
                return carry

            lax.fori_loop(0, z + 1, sent, 0)

        pair_copy(my_rows).wait_send()
        q_copy(my_rows).wait_send()

    @pl.when(seg == 0)
    def _state():
        me4 = tp * 2 + half
        get_x = pltpu.make_async_copy(x_hbm, xv, loc_sem.at[1])
        get_dt = pltpu.make_async_copy(wdt_hbm, wdtv, loc_sem.at[2])
        get_g = pltpu.make_async_copy(x_hbm.at[:, my_cols], xg.at[my_rows, :], loc_sem.at[3])
        quad = ((pair, 1 - tp), (z * 2 + half, 1 - tp), (pair, tp))
        groups = [t * 2 + c % 2 for c, t in quad] + [me4]

        def get_w(k, part):
            src = pl.ds(pl.multiple_of((part * GROUPS + groups[k]) * STATE, STATE), STATE)
            return pltpu.make_async_copy(
                w_hbm.at[:, src], wv.at[k, :, pl.ds(part * STATE, STATE)], w_sem.at[2 * k + part]
            )

        get_x.start()
        get_dt.start()
        for k in range(GROUPS):
            for part in range(2):
                get_w(k, part).start()
        get_g.start()
        for c, t in quad:
            signal(0, c, t)

        @pl.when(z > 0)
        def _():
            signal(0, ctx - 2, tp)

        more = jnp.where(z < nz - 1, 1, 0)
        pl.semaphore_wait(barrier, 3 + more)

        def x_copy(dst_rows):
            return remote(
                x_hbm.at[:, other_cols], xg.at[dst_rows, :], x_sem.at[0], x_sem.at[1], pair, tp
            )

        x_copy(my_rows).start()
        get_x.wait()
        get_dt.wait()
        x = xv[...]
        dt_all = dot_t(wdtv[...], x)
        psend_dt[...] = dt_all
        wide = x.astype(F32)
        sq_col = jnp.sum(wide * wide, axis=1, keepdims=True)
        sq_row = jnp.transpose(jnp.broadcast_to(sq_col, (ROWS, ROWS)))[0:8]

        def p_copy(k, slot):
            c, t = quad[k]
            return remote(psend.at[k], pbuf.at[slot], p_send.at[k], p_recv.at[k], c, t)

        for k in range(GROUPS):
            get_w(k, 0).wait()
            get_w(k, 1).wait()
            proj = dot(x, wv[k])
            dt_rows = pl.ds(pl.multiple_of(groups[k] * GHEADS, GHEADS), GHEADS)
            if k < 3:
                into = psend.at[k]
            else:
                into = pbuf.at[me4]
            into[0:ROWS] = proj[:, 0:STATE]
            into[ROWS : 2 * ROWS] = proj[:, STATE:]
            into[2 * ROWS : 2 * ROWS + GHEADS] = psend_dt[dt_rows]
            into[2 * ROWS + GHEADS : PACK] = sq_row
            if k < 3:
                p_copy(k, me4).start()
        for k in range(3):
            p_copy(k, groups[k]).wait_recv()

        span = 2 * ROWS
        r0 = pbuf[0] + pbuf[2]
        r1 = pbuf[1] + pbuf[3]
        b = jnp.concatenate([r0[0:ROWS], r1[0:ROWS]], axis=0)
        c_raw = jnp.concatenate([r0[ROWS : 2 * ROWS], r1[ROWS : 2 * ROWS]], axis=0)
        misc = jnp.concatenate([r0[2 * ROWS :], r1[2 * ROWS :]], axis=1)
        channels = 4 * GCOLS
        inv8 = lax.rsqrt(misc[GHEADS:MISC] / channels + EPSILON)
        inv = inv8[0:1]
        bias = head_column(bias_ref, half)
        rate = head_column(rate_ref, half)
        pre = misc[0:GHEADS] * inv + bias
        step = jnp.maximum(pre, 0.0) + jnp.log1p(jnp.exp(-jnp.abs(pre)))
        neg = -(step * rate)
        upto = (
            lax.broadcasted_iota(jnp.int32, (span, span), 0)
            <= lax.broadcasted_iota(jnp.int32, (span, span), 1)
        ).astype(F32).astype(BF16)
        n0 = neg.astype(BF16)
        rest = neg - n0.astype(F32)
        n1 = rest.astype(BF16)
        n2 = (rest - n1.astype(F32)).astype(BF16)
        log_decay = dot(n0, upto) + (dot(n1, upto) + dot(n2, upto))
        log_end = log_decay[:, span - 1 : span]
        u = step * inv
        root = math.sqrt(STATE)
        tall = jnp.concatenate(
            [
                log_decay,
                jnp.exp(log_end - log_decay) * u * inv,
                jnp.exp(log_decay) * inv / root,
                inv8,
                jnp.zeros((STATE - 3 * GHEADS - 8, span), F32),
            ],
            axis=0,
        )
        cols = jnp.transpose(tall)
        tcols[...] = cols
        rows_s[0] = log_decay
        rows_s[1] = u
        inv_col = cols[:, 3 * GHEADS : 3 * GHEADS + 1]
        bt_hi, bt_lo = split(jnp.transpose(b))
        c_hi, c_lo = split(c_raw)
        c_s[0] = c_hi
        c_s[1] = c_lo
        def columns(base, j):
            h = base + 2 * j
            return lane_pair(cols[:, h : h + 1], cols[:, h + 1 : h + 2], (span, 2 * SHEAD))

        def state_copy(j):
            return remote(
                s_out.at[j], s_in.at[j], st_send.at[j], st_recv.at[j],
                lax.rem(ctx + 2, 2 * nz), tp,
            )

        get_g.wait()
        x_copy(other_rows).wait_recv()
        for j in range(CHUNKS):
            xc = xg[:, j * CCOLS : (j + 1) * CCOLS].astype(F32)
            e = dot3((bt_hi, bt_lo), split(xc * columns(GHEADS, j)))
            ending[j] = e

            @pl.when(z == 0)
            def _():
                s_out[j] = e
                s_in[j] = jnp.zeros_like(e)
                state_copy(j).start()

        cb = dot3((c_hi, c_lo), (bt_hi, bt_lo)) * inv_col * inv / root
        lower = (
            lax.broadcasted_iota(jnp.int32, (span, span), 0)
            >= lax.broadcasted_iota(jnp.int32, (span, span), 1)
        )
        cb_s[...] = jnp.where(lower, cb, 0.0)

        last = cols[span - 8 : span][7:8]

        def pass_state(j):
            state_copy(j).wait_recv()

            @pl.when(z < nz - 1)
            def _():
                h = 2 * j
                fade = lane_pair(
                    jnp.exp(last[:, h : h + 1]), jnp.exp(last[:, h + 1 : h + 2]), (1, 2 * SHEAD)
                )
                s_out[j] = s_in[j] * fade + ending[j]
                state_copy(j).start()

        for j in range(CHUNKS):
            h = 2 * j
            xp = xg[:, h * SHEAD : (h + 2) * SHEAD]
            halves = []
            for d in range(2):
                lrow = rows_s[0, h + d : h + d + 1]
                urow = rows_s[1, h + d : h + d + 1]
                lcol = tcols[:, h + d : h + d + 1]
                top = (
                    jnp.exp(jnp.minimum(lcol[:ROWS] - lrow[:, :ROWS], 0.0))
                    * cb_s[:ROWS, :ROWS]
                    * urow[:, :ROWS]
                )
                low = jnp.exp(jnp.minimum(lcol[ROWS:] - lrow, 0.0)) * cb_s[ROWS:] * urow
                t_hi, t_lo = split(top)
                l_hi, l_lo = split(low)
                halves.append(
                    (
                        dot(t_hi, xp[:ROWS]) + dot(t_lo, xp[:ROWS]),
                        dot(l_hi, xp) + dot(l_lo, xp),
                    )
                )
            lane = lax.broadcasted_iota(jnp.int32, (ROWS, 2 * SHEAD), 1)
            at = slice(h * SHEAD, (h + 2) * SHEAD)
            local[0:ROWS, at] = jnp.where(lane < SHEAD, halves[0][0], halves[1][0])
            local[ROWS:span, at] = jnp.where(lane < SHEAD, halves[0][1], halves[1][1])

            @pl.when(z == 1)
            def _():
                pass_state(j)

        block = (
            lax.broadcasted_iota(jnp.int32, (CCOLS, CCOLS), 0) // SHEAD
            == lax.broadcasted_iota(jnp.int32, (CCOLS, CCOLS), 1) // SHEAD
        ).astype(F32).astype(BF16)

        def out_copy(j, base):
            at = pl.ds(pl.multiple_of(base * GCOLS + j * CCOLS, CCOLS), CCOLS)
            return remote(
                stage.at[other_rows, pl.ds(j * CCOLS, CCOLS)],
                out_ref.at[:, at],
                o_send.at[j],
                o_recv.at[j],
                pair,
                tp,
            )

        skip_row, gain_row = channel_rows(skip_ref, gain_ref, half)

        for j in range(CHUNKS):
            @pl.when(z > 1)
            def _():
                pass_state(j)

            at = slice(j * CCOLS, (j + 1) * CCOLS)
            xc = xg[:, at].astype(F32)
            inflow = dot3((c_s[0], c_s[1]), split(s_in[j]))
            gcols = pl.ds(pl.multiple_of(half * GCOLS + j * CCOLS, CCOLS), CCOLS)
            skip = skip_row[:, at]
            gain = gain_row[:, at]
            mixed = local[:, at] + inflow * columns(2 * GHEADS, j) + skip * (xc * inv_col)
            p_hi, p_lo = split(mixed * mixed)
            power = (dot(p_hi, block) + dot(p_lo, block)) / SHEAD
            stage[:, at] = (xc + gain * mixed * lax.rsqrt(power + EPSILON)).astype(BF16)
            out_copy(j, half).start()
            out_ref[:, gcols] = stage[my_rows, at]

        for j in range(CHUNKS):
            out_copy(j, half).wait_send()
            out_copy(j, other).wait_recv()

            @pl.when(z < nz - 1)
            def _():
                state_copy(j).wait_send()

        for k in range(3):
            p_copy(k, me4).wait_send()
        x_copy(my_rows).wait_send()


def body(queries, keys, values, layer_in, w_bc, w_dt, dt_bias, decay_rate, skip_gain, out_gain):
    nctx = lax.axis_size("ctx")
    nz = nctx // 2
    span = 2 * ROWS
    hbm_spec = pl.BlockSpec(memory_space=pltpu.HBM)
    vmem_spec = pl.BlockSpec(memory_space=pltpu.VMEM)
    dma = pltpu.SemaphoreType.DMA
    vm = pltpu.VMEM
    out = pl.pallas_call(
        functools.partial(kernel, nz),
        out_shape=jax.ShapeDtypeStruct(layer_in.shape, BF16),
        in_specs=[hbm_spec] * 6 + [vmem_spec] * 4,
        out_specs=vmem_spec,
        scratch_shapes=[
            vm(queries.shape, BF16),
            vm(keys.shape, BF16),
            vm(values.shape, BF16),
            vm((2, QH, ROWS, HEAD), BF16),
            vm((2, 4, ROWS, HEAD), BF16),
            vm((QH, span, HEAD), BF16),
            vm((nz, 4, span, HEAD), BF16),
            vm((nz, 2 * span, span), F32),
            vm(layer_in.shape, BF16),
            vm((GROUPS, w_bc.shape[1], 2 * STATE), BF16),
            vm((w_dt.shape[2], w_dt.shape[1]), BF16),
            vm((span, GCOLS), BF16),
            vm((GROUPS - 1, PACK, STATE), F32),
            vm((GROUPS * GHEADS, ROWS), F32),
            vm((GROUPS, PACK, STATE), F32),
            vm((span, STATE), F32),
            vm((2, GHEADS, span), F32),
            vm((8, STATE), BF16),
            vm((2, span, STATE), BF16),
            vm((span, span), F32),
            vm((CHUNKS, STATE, CCOLS), F32),
            vm((CHUNKS, STATE, CCOLS), F32),
            vm((CHUNKS, STATE, CCOLS), F32),
            vm((span, GCOLS), F32),
            vm((span, GCOLS), BF16),
            dma((4,)),
            dma((2 * GROUPS,)),
            dma((2,)),
            dma((2,)),
            dma((nz,)),
            dma((nz,)),
            dma((2,)),
            dma((3,)),
            dma((3,)),
            dma((CHUNKS,)),
            dma((CHUNKS,)),
            dma((CHUNKS,)),
            dma((CHUNKS,)),
        ],
        compiler_params=pltpu.CompilerParams(
            collective_id=0, has_side_effects=True, vmem_limit_bytes=60 * 1024 * 1024
        ),
    )(
        queries,
        keys,
        values,
        layer_in,
        w_bc[0],
        w_dt[0].T,
        dt_bias,
        decay_rate,
        skip_gain,
        out_gain[0],
    )
    return out[None]


def solution(mesh):
    in_specs = (
        P("ctx", "tp", None),
        P("ctx", "tp", None),
        P("ctx", "tp", None),
        P("ctx", "tp"),
        P(None, "tp", None),
        P(None, "tp", None),
        P(None, "tp"),
        P(None, "tp"),
        P(None, "tp"),
        P(None, "tp", None),
    )
    out_specs = P("segment", "ctx", "tp")
    return jax.shard_map(body, mesh=mesh, in_specs=in_specs, out_specs=out_specs, check_vma=False)
```

```python
import functools
import math

import jax
import jax.numpy as jnp
from jax import lax
from jax.experimental import pallas as pl
from jax.experimental.pallas import tpu as pltpu
from jax.sharding import PartitionSpec as P

MESH = pl.DeviceIdType.MESH
EPSILON = 1e-05
F32 = jnp.float32
BF16 = jnp.bfloat16

ROWS = 128
HEAD = 128
STATE = 128
SHEAD = 64
GHEADS = 16
GCOLS = GHEADS * SHEAD
GROUPS = 4
QH = 8
CHUNKS = 8
CCOLS = GCOLS // CHUNKS
MISC = 24
PACK = 2 * ROWS + MISC


def split(a):
    hi = a.astype(BF16)
    return hi, (a - hi.astype(F32)).astype(BF16)


def dot(a, b):
    return jnp.dot(a, b, preferred_element_type=F32)


def dot_t(a, b):
    return lax.dot_general(a, b, (((1,), (1,)), ((), ())), preferred_element_type=F32)


def dot3(a, b):
    return dot(a[0], b[0]) + (dot(a[0], b[1]) + dot(a[1], b[0]))


def dot3_t(a, b):
    return dot_t(a[0], b[0]) + (dot_t(a[0], b[1]) + dot_t(a[1], b[0]))


def lane_pair(left, right, shape):
    lane = lax.broadcasted_iota(jnp.int32, shape, 1)
    return jnp.where(lane < SHEAD, jnp.broadcast_to(left, shape), jnp.broadcast_to(right, shape))


def head_column(ref, half):
    shape = (GHEADS, ref.shape[1])
    wanted = lax.broadcasted_iota(jnp.int32, shape, 1) == (
        lax.broadcasted_iota(jnp.int32, shape, 0) + half * GHEADS
    )
    return jnp.sum(
        jnp.where(wanted, jnp.broadcast_to(ref[...], shape), 0.0), axis=1, keepdims=True
    )


def channel_rows(skip_ref, gain_ref, half):
    shape = (GHEADS, GCOLS)
    own = (
        lax.broadcasted_iota(jnp.int32, shape, 1) // SHEAD
        == lax.broadcasted_iota(jnp.int32, shape, 0)
    )
    skip = jnp.broadcast_to(head_column(skip_ref, half), shape)
    skip = jnp.sum(jnp.where(own, skip, 0.0), axis=0, keepdims=True)
    gain = gain_ref[pl.ds(pl.multiple_of(half * GHEADS, GHEADS), GHEADS), :]
    pairs = jnp.concatenate([gain, gain], axis=1)
    gain = jnp.concatenate([pairs] * (GHEADS // 2), axis=1)
    gain = jnp.sum(jnp.where(own, gain, 0.0), axis=0, keepdims=True)
    return skip, gain


def kernel(
    nz,
    q_hbm,
    k_hbm,
    v_hbm,
    x_hbm,
    w_hbm,
    wdt_hbm,
    bias_ref,
    rate_ref,
    skip_ref,
    gain_ref,
    out_ref,
    q_in,
    k_in,
    v_in,
    q_own,
    kv_own,
    qbuf,
    kvbuf,
    scores,
    xv,
    wv,
    wdtv,
    xg,
    psend,
    psend_dt,
    pbuf,
    tcols,
    rows_s,
    bt_s,
    c_s,
    cb_s,
    ending,
    s_in,
    s_out,
    local,
    stage,
    loc_sem,
    q_sem,
    pkv_sem,
    kv_send,
    kv_recv,
    x_sem,
    p_send,
    p_recv,
    st_send,
    st_recv,
    o_send,
    o_recv,
):
    seg = lax.axis_index("segment")
    ctx = lax.axis_index("ctx")
    tp = lax.axis_index("tp")
    z = ctx // 2
    half = ctx % 2
    other = 1 - half
    pair = z * 2 + other
    barrier = pltpu.get_barrier_semaphore()
    my_rows = pl.ds(pl.multiple_of(half * ROWS, ROWS), ROWS)
    other_rows = pl.ds(pl.multiple_of(other * ROWS, ROWS), ROWS)
    my_cols = pl.ds(pl.multiple_of(half * GCOLS, GCOLS), GCOLS)
    other_cols = pl.ds(pl.multiple_of(other * GCOLS, GCOLS), GCOLS)

    def signal(s, c, t):
        pl.semaphore_signal(barrier, inc=1, device_id=(s, c, t), device_id_type=MESH)

    def remote(src, dst, send, recv, c, t):
        return pltpu.make_async_remote_copy(
            src_ref=src,
            dst_ref=dst,
            send_sem=send,
            recv_sem=recv,
            device_id=(seg, c, t),
            device_id_type=MESH,
        )

    @pl.when(seg == 1)
    def _attention():
        get_k = pltpu.make_async_copy(k_hbm, k_in, loc_sem.at[0])
        get_v = pltpu.make_async_copy(v_hbm, v_in, loc_sem.at[1])
        get_q = pltpu.make_async_copy(q_hbm, q_in, loc_sem.at[2])
        get_k.start()
        get_v.start()
        get_q.start()
        signal(1, pair, tp)

        @pl.when(z > 0)
        def _():
            signal(1, ctx - 2, tp)

        get_k.wait()
        get_v.wait()
        k_heads = jnp.swapaxes(k_in[...].astype(F32), 0, 1).astype(BF16)
        v_heads = jnp.swapaxes(v_in[...].astype(F32), 0, 1).astype(BF16)
        for p in range(2):
            kv_own[p, 0:2] = k_heads[2 * p : 2 * p + 2]
            kv_own[p, 2:4] = v_heads[2 * p : 2 * p + 2]
        pl.semaphore_wait(barrier, 1 + jnp.where(z < nz - 1, 1, 0))
        following = lax.rem(ctx + 2, 2 * nz)

        def pair_copy(dst_rows):
            return remote(
                kv_own.at[other], kvbuf.at[z, :, dst_rows, :], pkv_sem.at[0], pkv_sem.at[1], pair, tp
            )

        def pass_on(zz, part):
            block = kvbuf.at[zz, pl.ds(2 * part, 2)]
            at = 2 * zz + part
            return remote(block, block, kv_send.at[at], kv_recv.at[at], following, tp)

        def q_copy(dst_rows):
            return remote(
                q_own.at[other], qbuf.at[:, dst_rows, :], q_sem.at[0], q_sem.at[1], pair, tp
            )

        pair_copy(my_rows).start()
        kvbuf[z, :, my_rows, :] = kv_own[half]
        get_q.wait()
        q_own[...] = (
            jnp.swapaxes(q_in[...].astype(F32), 0, 1).astype(BF16).reshape(2, QH, ROWS, HEAD)
        )
        qbuf[:, my_rows, :] = q_own[half]
        pair_copy(other_rows).wait_recv()

        @pl.when(z < nz - 1)
        def _():
            pass_on(z, 0).start()
            pass_on(z, 1).start()

        q_copy(my_rows).start()

        def arrive(k, carry):
            zz = z - 1 - k
            for part in range(2):
                pass_on(zz, part).wait_recv()

                @pl.when(z < nz - 1)
                def _():
                    pass_on(zz, part).start()

            return carry

        lax.fori_loop(0, z, arrive, 0)
        q_copy(other_rows).wait_recv()
        scale = 1.0 / math.sqrt(HEAD)
        span = 2 * ROWS
        rows2 = 2 * span
        t_at = lax.broadcasted_iota(jnp.int32, (rows2, span), 0) % span
        s_at = lax.broadcasted_iota(jnp.int32, (rows2, span), 1)
        allowed = t_at >= s_at

        def two_heads(i, carry):
            kvh = i // 2
            q = qbuf[pl.ds(i * 2, 2)].reshape(rows2, HEAD)
            diag = dot_t(q, kvbuf[z, kvh]) * scale
            diag = jnp.where(allowed, diag, -1e30)

            def first(zz, top):
                s = dot_t(q, kvbuf[zz, kvh]) * scale
                scores[zz] = s
                return jnp.maximum(top, jnp.max(s, axis=1, keepdims=True))

            top = lax.fori_loop(0, z, first, jnp.max(diag, axis=1, keepdims=True))
            weight = jnp.exp(diag - top)
            total = jnp.sum(weight, axis=1, keepdims=True)
            acc = dot(weight.astype(BF16), kvbuf[z, kvh + 2])

            def second(zz, kept):
                total, acc = kept
                weight = jnp.exp(scores[zz] - top)
                return (
                    total + jnp.sum(weight, axis=1, keepdims=True),
                    acc + dot(weight.astype(BF16), kvbuf[zz, kvh + 2]),
                )

            total, acc = lax.fori_loop(0, z, second, (total, acc))
            done = (acc / total).astype(BF16)
            for k in range(2):
                cols = pl.ds(pl.multiple_of((i * 2 + k) * HEAD, HEAD), HEAD)
                stage[:, cols] = done[k * span : (k + 1) * span]
            at = pl.ds(pl.multiple_of(i * 2 * HEAD, 2 * HEAD), 2 * HEAD)
            to = pl.ds(pl.multiple_of(half * GCOLS + i * 2 * HEAD, 2 * HEAD), 2 * HEAD)
            out_copy(i, half).start()
            out_ref[:, to] = stage[my_rows, at]
            return carry

        def out_copy(i, base):
            at = pl.ds(pl.multiple_of(i * 2 * HEAD, 2 * HEAD), 2 * HEAD)
            to = pl.ds(pl.multiple_of(base * GCOLS + i * 2 * HEAD, 2 * HEAD), 2 * HEAD)
            return remote(
                stage.at[other_rows, at], out_ref.at[:, to], o_send.at[i], o_recv.at[i], pair, tp
            )

        lax.fori_loop(0, QH // 2, two_heads, 0)
        for i in range(QH // 2):
            out_copy(i, half).wait_send()
            out_copy(i, other).wait_recv()

        @pl.when(z < nz - 1)
        def _():
            def sent(zz, carry):
                pass_on(zz, 0).wait_send()
                pass_on(zz, 1).wait_send()
                return carry

            lax.fori_loop(0, z + 1, sent, 0)

        pair_copy(my_rows).wait_send()
        q_copy(my_rows).wait_send()

    @pl.when(seg == 0)
    def _state():
        me4 = tp * 2 + half
        get_x = pltpu.make_async_copy(x_hbm, xv, loc_sem.at[1])
        get_dt = pltpu.make_async_copy(wdt_hbm, wdtv, loc_sem.at[2])
        get_g = pltpu.make_async_copy(x_hbm.at[:, my_cols], xg.at[my_rows, :], loc_sem.at[3])
        quad = ((pair, 1 - tp), (z * 2 + half, 1 - tp), (pair, tp))
        groups = [t * 2 + c % 2 for c, t in quad] + [me4]

        get_w = pltpu.make_async_copy(w_hbm, wv, loc_sem.at[0])
        get_w.start()
        get_x.start()
        get_dt.start()
        get_g.start()
        for c, t in quad:
            signal(0, c, t)

        @pl.when(z > 0)
        def _():
            signal(0, ctx - 2, tp)

        more = jnp.where(z < nz - 1, 1, 0)
        pl.semaphore_wait(barrier, 3 + more)

        def x_copy(dst_rows):
            return remote(
                x_hbm.at[:, other_cols], xg.at[dst_rows, :], x_sem.at[0], x_sem.at[1], pair, tp
            )

        get_x.wait()
        get_dt.wait()
        x = xv[...]
        dt_all = dot_t(wdtv[...], x)
        psend_dt[...] = dt_all
        wide = x.astype(F32)
        sq_col = jnp.sum(wide * wide, axis=1, keepdims=True)
        sq_row = jnp.transpose(jnp.broadcast_to(sq_col, (ROWS, ROWS)))[0:8]

        def p_copy(k, slot):
            c, t = quad[k]
            return remote(psend.at[k], pbuf.at[slot], p_send.at[k], p_recv.at[k], c, t)

        x_copy(my_rows).start()
        get_w.wait()
        for k in range(GROUPS):
            at_b = pl.ds(pl.multiple_of(groups[k] * STATE, STATE), STATE)
            at_c = pl.ds(pl.multiple_of((GROUPS + groups[k]) * STATE, STATE), STATE)
            proj = dot(x, jnp.concatenate([wv[:, at_b], wv[:, at_c]], axis=1))
            dt_rows = pl.ds(pl.multiple_of(groups[k] * GHEADS, GHEADS), GHEADS)
            if k < 3:
                into = psend.at[k]
            else:
                into = pbuf.at[me4]
            into[0:ROWS] = proj[:, 0:STATE]
            into[ROWS : 2 * ROWS] = proj[:, STATE:]
            into[2 * ROWS : 2 * ROWS + GHEADS] = psend_dt[dt_rows]
            into[2 * ROWS + GHEADS : PACK] = sq_row
            if k < 3:
                p_copy(k, me4).start()
        for k in range(3):
            p_copy(k, groups[k]).wait_recv()

        span = 2 * ROWS
        r0 = pbuf[0] + pbuf[2]
        r1 = pbuf[1] + pbuf[3]
        b = jnp.concatenate([r0[0:ROWS], r1[0:ROWS]], axis=0)
        c_raw = jnp.concatenate([r0[ROWS : 2 * ROWS], r1[ROWS : 2 * ROWS]], axis=0)
        misc = jnp.concatenate([r0[2 * ROWS :], r1[2 * ROWS :]], axis=1)
        channels = 4 * GCOLS
        inv8 = lax.rsqrt(misc[GHEADS:MISC] / channels + EPSILON)
        inv = inv8[0:1]
        bias = head_column(bias_ref, half)
        rate = head_column(rate_ref, half)
        pre = misc[0:GHEADS] * inv + bias
        step = jnp.maximum(pre, 0.0) + jnp.log1p(jnp.exp(-jnp.abs(pre)))
        neg = -(step * rate)
        upto = (
            lax.broadcasted_iota(jnp.int32, (span, span), 0)
            <= lax.broadcasted_iota(jnp.int32, (span, span), 1)
        ).astype(F32).astype(BF16)
        n0 = neg.astype(BF16)
        rest = neg - n0.astype(F32)
        n1 = rest.astype(BF16)
        n2 = (rest - n1.astype(F32)).astype(BF16)
        log_decay = dot(n0, upto) + (dot(n1, upto) + dot(n2, upto))
        log_end = log_decay[:, span - 1 : span]
        u = step * inv
        root = math.sqrt(STATE)
        tall = jnp.concatenate(
            [
                log_decay,
                jnp.exp(log_end - log_decay) * u * inv,
                jnp.exp(log_decay) * inv / root,
                inv8,
                jnp.zeros((STATE - 3 * GHEADS - 8, span), F32),
            ],
            axis=0,
        )
        cols = jnp.transpose(tall)
        tcols[...] = cols
        rows_s[0] = log_decay
        rows_s[1] = u
        inv_col = cols[:, 3 * GHEADS : 3 * GHEADS + 1]
        bt_hi, bt_lo = split(jnp.transpose(b))
        c_hi, c_lo = split(c_raw)
        c_s[0] = c_hi
        c_s[1] = c_lo
        def columns(base, j):
            h = base + 2 * j
            return lane_pair(cols[:, h : h + 1], cols[:, h + 1 : h + 2], (span, 2 * SHEAD))

        following = lax.rem(ctx + 2, 2 * nz)

        def first_copy(j):
            return remote(ending.at[j], s_in.at[j], st_send.at[j], st_recv.at[j], following, tp)

        def state_copy(j):
            return remote(s_out.at[j], s_in.at[j], st_send.at[j], st_recv.at[j], following, tp)

        get_g.wait()
        x_copy(other_rows).wait_recv()
        for j in range(CHUNKS):
            xc = xg[:, j * CCOLS : (j + 1) * CCOLS].astype(F32)
            e = dot3((bt_hi, bt_lo), split(xc * columns(GHEADS, j)))
            ending[j] = e

        @pl.when(z == 0)
        def _():
            for j in range(CHUNKS):
                first_copy(j).start()

        @pl.when(z == 0)
        def _():
            s_in[...] = jnp.zeros_like(s_in)

        cb = dot3((c_hi, c_lo), (bt_hi, bt_lo)) * inv_col * inv / root
        lower = (
            lax.broadcasted_iota(jnp.int32, (span, span), 0)
            >= lax.broadcasted_iota(jnp.int32, (span, span), 1)
        )
        cb_s[...] = jnp.where(lower, cb, 0.0)

        last = cols[span - 8 : span][7:8]
        skip_row, gain_row = channel_rows(skip_ref, gain_ref, half)

        def pass_state(j):
            state_copy(j).wait_recv()

            @pl.when(z < nz - 1)
            def _():
                h = 2 * j
                fade = lane_pair(
                    jnp.exp(last[:, h : h + 1]), jnp.exp(last[:, h + 1 : h + 2]), (1, 2 * SHEAD)
                )
                s_out[j] = s_in[j] * fade + ending[j]
                state_copy(j).start()

        for j in range(CHUNKS):
            h = 2 * j
            xp = xg[:, h * SHEAD : (h + 2) * SHEAD]
            halves = []
            for d in range(2):
                lrow = rows_s[0, h + d : h + d + 1]
                urow = rows_s[1, h + d : h + d + 1]
                lcol = tcols[:, h + d : h + d + 1]
                top = (
                    jnp.exp(jnp.minimum(lcol[:ROWS] - lrow[:, :ROWS], 0.0))
                    * cb_s[:ROWS, :ROWS]
                    * urow[:, :ROWS]
                )
                low = jnp.exp(jnp.minimum(lcol[ROWS:] - lrow, 0.0)) * cb_s[ROWS:] * urow
                t_hi, t_lo = split(top)
                l_hi, l_lo = split(low)
                halves.append(
                    (
                        dot(t_hi, xp[:ROWS]) + dot(t_lo, xp[:ROWS]),
                        dot(l_hi, xp) + dot(l_lo, xp),
                    )
                )
            lane = lax.broadcasted_iota(jnp.int32, (ROWS, 2 * SHEAD), 1)
            at = slice(h * SHEAD, (h + 2) * SHEAD)
            local[0:ROWS, at] = jnp.where(lane < SHEAD, halves[0][0], halves[1][0])
            local[ROWS:span, at] = jnp.where(lane < SHEAD, halves[0][1], halves[1][1])

            if j % 2 == 1:

                @pl.when(z == 1)
                def _():
                    pass_state(j - 1)
                    pass_state(j)

        block = (
            lax.broadcasted_iota(jnp.int32, (CCOLS, CCOLS), 0) // SHEAD
            == lax.broadcasted_iota(jnp.int32, (CCOLS, CCOLS), 1) // SHEAD
        ).astype(F32).astype(BF16)

        def out_copy(i, base):
            at = pl.ds(pl.multiple_of(base * GCOLS + 2 * i * CCOLS, 2 * CCOLS), 2 * CCOLS)
            return remote(
                stage.at[other_rows, pl.ds(2 * i * CCOLS, 2 * CCOLS)],
                out_ref.at[:, at],
                o_send.at[i],
                o_recv.at[i],
                pair,
                tp,
            )

        for j in range(CHUNKS):
            if j % 2 == 0:

                @pl.when(z > 1)
                def _():
                    pass_state(j)
                    pass_state(j + 1)

            at = slice(j * CCOLS, (j + 1) * CCOLS)
            xc = xg[:, at].astype(F32)
            inflow = dot3((c_s[0], c_s[1]), split(s_in[j]))
            skip = skip_row[:, at]
            gain = gain_row[:, at]
            mixed = local[:, at] + inflow * columns(2 * GHEADS, j) + skip * (xc * inv_col)
            p_hi, p_lo = split(mixed * mixed)
            power = (dot(p_hi, block) + dot(p_lo, block)) / SHEAD
            stage[:, at] = (xc + gain * mixed * lax.rsqrt(power + EPSILON)).astype(BF16)
            if j % 2 == 1:
                out_copy(j // 2, half).start()
                two = slice((j - 1) * CCOLS, (j + 1) * CCOLS)
                out_ref[:, pl.ds(pl.multiple_of(half * GCOLS + (j - 1) * CCOLS, 2 * CCOLS), 2 * CCOLS)] = (
                    stage[my_rows, two]
                )

        for j in range(CHUNKS):
            if j % 2 == 1:
                out_copy(j // 2, half).wait_send()
                out_copy(j // 2, other).wait_recv()

        @pl.when(z < nz - 1)
        def _():
            for j in range(CHUNKS):
                state_copy(j).wait_send()

        for k in range(3):
            p_copy(k, me4).wait_send()
        x_copy(my_rows).wait_send()


def body(queries, keys, values, layer_in, w_bc, w_dt, dt_bias, decay_rate, skip_gain, out_gain):
    nctx = lax.axis_size("ctx")
    nz = nctx // 2
    span = 2 * ROWS
    hbm_spec = pl.BlockSpec(memory_space=pltpu.HBM)
    vmem_spec = pl.BlockSpec(memory_space=pltpu.VMEM)
    dma = pltpu.SemaphoreType.DMA
    vm = pltpu.VMEM
    out = pl.pallas_call(
        functools.partial(kernel, nz),
        out_shape=jax.ShapeDtypeStruct(layer_in.shape, BF16),
        in_specs=[hbm_spec] * 6 + [vmem_spec] * 4,
        out_specs=vmem_spec,
        scratch_shapes=[
            vm(queries.shape, BF16),
            vm(keys.shape, BF16),
            vm(values.shape, BF16),
            vm((2, QH, ROWS, HEAD), BF16),
            vm((2, 4, ROWS, HEAD), BF16),
            vm((QH, span, HEAD), BF16),
            vm((nz, 4, span, HEAD), BF16),
            vm((nz, 2 * span, span), F32),
            vm(layer_in.shape, BF16),
            vm(w_bc.shape[1:], BF16),
            vm((w_dt.shape[2], w_dt.shape[1]), BF16),
            vm((span, GCOLS), BF16),
            vm((GROUPS - 1, PACK, STATE), F32),
            vm((GROUPS * GHEADS, ROWS), F32),
            vm((GROUPS, PACK, STATE), F32),
            vm((span, STATE), F32),
            vm((2, GHEADS, span), F32),
            vm((8, STATE), BF16),
            vm((2, span, STATE), BF16),
            vm((span, span), F32),
            vm((CHUNKS, STATE, CCOLS), F32),
            vm((CHUNKS, STATE, CCOLS), F32),
            vm((CHUNKS, STATE, CCOLS), F32),
            vm((span, GCOLS), F32),
            vm((span, GCOLS), BF16),
            dma((4,)),
            dma((2,)),
            dma((2,)),
            dma((2 * nz,)),
            dma((2 * nz,)),
            dma((2,)),
            dma((3,)),
            dma((3,)),
            dma((CHUNKS,)),
            dma((CHUNKS,)),
            dma((CHUNKS,)),
            dma((CHUNKS,)),
        ],
        compiler_params=pltpu.CompilerParams(
            collective_id=0, has_side_effects=True, vmem_limit_bytes=60 * 1024 * 1024
        ),
    )(
        queries,
        keys,
        values,
        layer_in,
        w_bc[0],
        w_dt[0].T,
        dt_bias,
        decay_rate,
        skip_gain,
        out_gain[0],
    )
    return out[None]


def solution(mesh):
    in_specs = (
        P("ctx", "tp", None),
        P("ctx", "tp", None),
        P("ctx", "tp", None),
        P("ctx", "tp"),
        P(None, "tp", None),
        P(None, "tp", None),
        P(None, "tp"),
        P(None, "tp"),
        P(None, "tp"),
        P(None, "tp", None),
    )
    out_specs = P("segment", "ctx", "tp")
    return jax.shard_map(body, mesh=mesh, in_specs=in_specs, out_specs=out_specs, check_vma=False)
```

```python
import functools
import math

import jax
import jax.numpy as jnp
from jax import lax
from jax.experimental import pallas as pl
from jax.experimental.pallas import tpu as pltpu
from jax.sharding import PartitionSpec as P

MESH = pl.DeviceIdType.MESH
EPSILON = 1e-05
F32 = jnp.float32
BF16 = jnp.bfloat16

ROWS = 128
HEAD = 128
STATE = 128
SHEAD = 64
GHEADS = 16
GCOLS = GHEADS * SHEAD
GROUPS = 4
QH = 8
CHUNKS = 8
CCOLS = GCOLS // CHUNKS
MISC = 24
PACK = 2 * ROWS + MISC


def split(a):
    hi = a.astype(BF16)
    return hi, (a - hi.astype(F32)).astype(BF16)


def dot(a, b):
    return jnp.dot(a, b, preferred_element_type=F32)


def dot_t(a, b):
    return lax.dot_general(a, b, (((1,), (1,)), ((), ())), preferred_element_type=F32)


def dot3(a, b):
    return dot(a[0], b[0]) + (dot(a[0], b[1]) + dot(a[1], b[0]))


def dot3_t(a, b):
    return dot_t(a[0], b[0]) + (dot_t(a[0], b[1]) + dot_t(a[1], b[0]))


def lane_pair(left, right, shape):
    lane = lax.broadcasted_iota(jnp.int32, shape, 1)
    return jnp.where(lane < SHEAD, jnp.broadcast_to(left, shape), jnp.broadcast_to(right, shape))


def head_column(ref, half):
    shape = (GHEADS, ref.shape[1])
    wanted = lax.broadcasted_iota(jnp.int32, shape, 1) == (
        lax.broadcasted_iota(jnp.int32, shape, 0) + half * GHEADS
    )
    return jnp.sum(
        jnp.where(wanted, jnp.broadcast_to(ref[...], shape), 0.0), axis=1, keepdims=True
    )


def channel_rows(skip_ref, gain_ref, half):
    shape = (GHEADS, GCOLS)
    own = (
        lax.broadcasted_iota(jnp.int32, shape, 1) // SHEAD
        == lax.broadcasted_iota(jnp.int32, shape, 0)
    )
    skip = jnp.broadcast_to(head_column(skip_ref, half), shape)
    skip = jnp.sum(jnp.where(own, skip, 0.0), axis=0, keepdims=True)
    gain = gain_ref[pl.ds(pl.multiple_of(half * GHEADS, GHEADS), GHEADS), :]
    pairs = jnp.concatenate([gain, gain], axis=1)
    gain = jnp.concatenate([pairs] * (GHEADS // 2), axis=1)
    gain = jnp.sum(jnp.where(own, gain, 0.0), axis=0, keepdims=True)
    return skip, gain


def kernel(
    nz,
    q_hbm,
    k_hbm,
    v_hbm,
    x_hbm,
    w_hbm,
    wdt_hbm,
    bias_ref,
    rate_ref,
    skip_ref,
    gain_ref,
    out_ref,
    q_in,
    k_in,
    v_in,
    q_own,
    kv_own,
    qbuf,
    kvbuf,
    scores,
    xv,
    wv,
    wdtv,
    xg,
    psend,
    psend_dt,
    pbuf,
    tcols,
    rows_s,
    bt_s,
    c_s,
    cb_s,
    ending,
    s_in,
    s_out,
    local,
    stage,
    loc_sem,
    q_sem,
    pkv_sem,
    kv_send,
    kv_recv,
    x_sem,
    p_send,
    p_recv,
    st_send,
    st_recv,
    o_send,
    o_recv,
):
    seg = lax.axis_index("segment")
    ctx = lax.axis_index("ctx")
    tp = lax.axis_index("tp")
    z = ctx // 2
    half = ctx % 2
    other = 1 - half
    pair = z * 2 + other
    barrier = pltpu.get_barrier_semaphore()
    my_rows = pl.ds(pl.multiple_of(half * ROWS, ROWS), ROWS)
    other_rows = pl.ds(pl.multiple_of(other * ROWS, ROWS), ROWS)
    my_cols = pl.ds(pl.multiple_of(half * GCOLS, GCOLS), GCOLS)
    other_cols = pl.ds(pl.multiple_of(other * GCOLS, GCOLS), GCOLS)

    def signal(s, c, t):
        pl.semaphore_signal(barrier, inc=1, device_id=(s, c, t), device_id_type=MESH)

    def remote(src, dst, send, recv, c, t):
        return pltpu.make_async_remote_copy(
            src_ref=src,
            dst_ref=dst,
            send_sem=send,
            recv_sem=recv,
            device_id=(seg, c, t),
            device_id_type=MESH,
        )

    @pl.when(seg == 1)
    def _attention():
        get_k = pltpu.make_async_copy(k_hbm, k_in, loc_sem.at[0])
        get_v = pltpu.make_async_copy(v_hbm, v_in, loc_sem.at[1])
        get_q = pltpu.make_async_copy(q_hbm, q_in, loc_sem.at[2])
        get_k.start()
        get_v.start()
        get_q.start()
        signal(1, pair, tp)

        @pl.when(z > 0)
        def _():
            signal(1, ctx - 2, tp)

        get_k.wait()
        get_v.wait()
        k_heads = jnp.swapaxes(k_in[...].astype(F32), 0, 1).astype(BF16)
        v_heads = jnp.swapaxes(v_in[...].astype(F32), 0, 1).astype(BF16)
        for p in range(2):
            kv_own[p, 0:2] = k_heads[2 * p : 2 * p + 2]
            kv_own[p, 2:4] = v_heads[2 * p : 2 * p + 2]
        pl.semaphore_wait(barrier, 1 + jnp.where(z < nz - 1, 1, 0))
        following = lax.rem(ctx + 2, 2 * nz)

        def pair_copy(dst_rows):
            return remote(
                kv_own.at[other], kvbuf.at[z, :, dst_rows, :], pkv_sem.at[0], pkv_sem.at[1], pair, tp
            )

        def pass_on(zz, part):
            block = kvbuf.at[zz, pl.ds(2 * part, 2)]
            at = 2 * zz + part
            return remote(block, block, kv_send.at[at], kv_recv.at[at], following, tp)

        def q_copy(dst_rows):
            return remote(
                q_own.at[other], qbuf.at[:, dst_rows, :], q_sem.at[0], q_sem.at[1], pair, tp
            )

        pair_copy(my_rows).start()
        kvbuf[z, :, my_rows, :] = kv_own[half]
        get_q.wait()
        q_own[...] = (
            jnp.swapaxes(q_in[...].astype(F32), 0, 1).astype(BF16).reshape(2, QH, ROWS, HEAD)
        )
        qbuf[:, my_rows, :] = q_own[half]
        pair_copy(other_rows).wait_recv()

        @pl.when(z < nz - 1)
        def _():
            pass_on(z, 0).start()
            pass_on(z, 1).start()

        @pl.when(z < nz - 1)
        def _():
            pass_on(z, 0).wait_send()
            pass_on(z, 1).wait_send()
            q_copy(my_rows).start()

        def arrive(k, carry):
            zz = z - 1 - k
            for part in range(2):
                pass_on(zz, part).wait_recv()

                @pl.when(z < nz - 1)
                def _():
                    pass_on(zz, part).start()

            @pl.when(jnp.logical_and(z == nz - 1, k == 0))
            def _():
                q_copy(my_rows).start()

            return carry

        lax.fori_loop(0, z, arrive, 0)
        q_copy(other_rows).wait_recv()
        scale = 1.0 / math.sqrt(HEAD)
        span = 2 * ROWS
        rows2 = 2 * span
        t_at = lax.broadcasted_iota(jnp.int32, (rows2, span), 0) % span
        s_at = lax.broadcasted_iota(jnp.int32, (rows2, span), 1)
        allowed = t_at >= s_at

        def two_heads(i, carry):
            kvh = i // 2
            q = qbuf[pl.ds(i * 2, 2)].reshape(rows2, HEAD)
            diag = dot_t(q, kvbuf[z, kvh]) * scale
            diag = jnp.where(allowed, diag, -1e30)

            def first(zz, top):
                s = dot_t(q, kvbuf[zz, kvh]) * scale
                scores[zz] = s
                return jnp.maximum(top, jnp.max(s, axis=1, keepdims=True))

            top = lax.fori_loop(0, z, first, jnp.max(diag, axis=1, keepdims=True))
            weight = jnp.exp(diag - top)
            total = jnp.sum(weight, axis=1, keepdims=True)
            acc = dot(weight.astype(BF16), kvbuf[z, kvh + 2])

            def second(zz, kept):
                total, acc = kept
                weight = jnp.exp(scores[zz] - top)
                return (
                    total + jnp.sum(weight, axis=1, keepdims=True),
                    acc + dot(weight.astype(BF16), kvbuf[zz, kvh + 2]),
                )

            total, acc = lax.fori_loop(0, z, second, (total, acc))
            done = (acc / total).astype(BF16)
            for k in range(2):
                cols = pl.ds(pl.multiple_of((i * 2 + k) * HEAD, HEAD), HEAD)
                stage[:, cols] = done[k * span : (k + 1) * span]
            at = pl.ds(pl.multiple_of(i * 2 * HEAD, 2 * HEAD), 2 * HEAD)
            to = pl.ds(pl.multiple_of(half * GCOLS + i * 2 * HEAD, 2 * HEAD), 2 * HEAD)
            out_copy(i, half).start()
            out_ref[:, to] = stage[my_rows, at]
            return carry

        def out_copy(i, base):
            at = pl.ds(pl.multiple_of(i * 2 * HEAD, 2 * HEAD), 2 * HEAD)
            to = pl.ds(pl.multiple_of(base * GCOLS + i * 2 * HEAD, 2 * HEAD), 2 * HEAD)
            return remote(
                stage.at[other_rows, at], out_ref.at[:, to], o_send.at[i], o_recv.at[i], pair, tp
            )

        lax.fori_loop(0, QH // 2, two_heads, 0)
        for i in range(QH // 2):
            out_copy(i, half).wait_send()
            out_copy(i, other).wait_recv()

        @pl.when(z < nz - 1)
        def _():
            def sent(zz, carry):
                pass_on(zz, 0).wait_send()
                pass_on(zz, 1).wait_send()
                return carry

            lax.fori_loop(0, z, sent, 0)

        pair_copy(my_rows).wait_send()
        q_copy(my_rows).wait_send()

    @pl.when(seg == 0)
    def _state():
        me4 = tp * 2 + half
        get_x = pltpu.make_async_copy(x_hbm, xv, loc_sem.at[1])
        get_dt = pltpu.make_async_copy(wdt_hbm, wdtv, loc_sem.at[2])
        get_g = pltpu.make_async_copy(x_hbm.at[:, my_cols], xg.at[my_rows, :], loc_sem.at[3])
        quad = ((pair, 1 - tp), (z * 2 + half, 1 - tp), (pair, tp))
        groups = [t * 2 + c % 2 for c, t in quad] + [me4]

        get_w = pltpu.make_async_copy(w_hbm, wv, loc_sem.at[0])
        get_w.start()
        get_x.start()
        get_dt.start()
        get_g.start()
        for c, t in quad:
            signal(0, c, t)

        @pl.when(z > 0)
        def _():
            signal(0, ctx - 2, tp)

        more = jnp.where(z < nz - 1, 1, 0)
        pl.semaphore_wait(barrier, 3 + more)

        def x_copy(dst_rows):
            return remote(
                x_hbm.at[:, other_cols], xg.at[dst_rows, :], x_sem.at[0], x_sem.at[1], pair, tp
            )

        x_copy(my_rows).start()
        get_x.wait()
        get_dt.wait()
        x = xv[...]
        dt_all = dot_t(x, wdtv[...])
        dt_all = jnp.concatenate([dt_all, jnp.zeros_like(dt_all)], axis=1)
        psend_dt[...] = jnp.transpose(dt_all)[0 : GROUPS * GHEADS]
        wide = x.astype(F32)
        sq_col = jnp.sum(wide * wide, axis=1, keepdims=True)
        sq_row = jnp.transpose(jnp.broadcast_to(sq_col, (ROWS, ROWS)))[0:8]

        def p_copy(k, slot):
            c, t = quad[k]
            return remote(psend.at[k], pbuf.at[slot], p_send.at[k], p_recv.at[k], c, t)

        get_w.wait()
        for k in range(GROUPS):
            at_b = pl.ds(pl.multiple_of(groups[k] * STATE, STATE), STATE)
            at_c = pl.ds(pl.multiple_of((GROUPS + groups[k]) * STATE, STATE), STATE)
            proj = dot(x, jnp.concatenate([wv[:, at_b], wv[:, at_c]], axis=1))
            dt_rows = pl.ds(pl.multiple_of(groups[k] * GHEADS, GHEADS), GHEADS)
            if k < 3:
                into = psend.at[k]
            else:
                into = pbuf.at[me4]
            into[0:ROWS] = proj[:, 0:STATE]
            into[ROWS : 2 * ROWS] = proj[:, STATE:]
            into[2 * ROWS : 2 * ROWS + GHEADS] = psend_dt[dt_rows]
            into[2 * ROWS + GHEADS : PACK] = sq_row
            if k < 3:
                p_copy(k, me4).start()
        for k in range(3):
            p_copy(k, groups[k]).wait_recv()

        span = 2 * ROWS
        r0 = pbuf[0] + pbuf[2]
        r1 = pbuf[1] + pbuf[3]
        b = jnp.concatenate([r0[0:ROWS], r1[0:ROWS]], axis=0)
        c_raw = jnp.concatenate([r0[ROWS : 2 * ROWS], r1[ROWS : 2 * ROWS]], axis=0)
        misc = jnp.concatenate([r0[2 * ROWS :], r1[2 * ROWS :]], axis=1)
        channels = 4 * GCOLS
        inv8 = lax.rsqrt(misc[GHEADS:MISC] / channels + EPSILON)
        inv = inv8[0:1]
        bias = head_column(bias_ref, half)
        rate = head_column(rate_ref, half)
        pre = misc[0:GHEADS] * inv + bias
        step = jnp.maximum(pre, 0.0) + jnp.log1p(jnp.exp(-jnp.abs(pre)))
        neg = -(step * rate)
        upto = (
            lax.broadcasted_iota(jnp.int32, (span, span), 0)
            <= lax.broadcasted_iota(jnp.int32, (span, span), 1)
        ).astype(F32).astype(BF16)
        n0 = neg.astype(BF16)
        rest = neg - n0.astype(F32)
        n1 = rest.astype(BF16)
        n2 = (rest - n1.astype(F32)).astype(BF16)
        log_decay = dot(n0, upto) + (dot(n1, upto) + dot(n2, upto))
        log_end = log_decay[:, span - 1 : span]
        u = step * inv
        root = math.sqrt(STATE)
        tall = jnp.concatenate(
            [
                log_decay,
                jnp.exp(log_end - log_decay) * u * inv,
                jnp.exp(log_decay) * inv / root,
                inv8,
                jnp.zeros((STATE - 3 * GHEADS - 8, span), F32),
            ],
            axis=0,
        )
        cols = jnp.transpose(tall)
        tcols[...] = cols
        rows_s[0] = log_decay
        rows_s[1] = u
        inv_col = cols[:, 3 * GHEADS : 3 * GHEADS + 1]
        bt_hi, bt_lo = split(jnp.transpose(b))
        c_hi, c_lo = split(c_raw)
        c_s[0] = c_hi
        c_s[1] = c_lo
        def columns(base, j):
            h = base + 2 * j
            return lane_pair(cols[:, h : h + 1], cols[:, h + 1 : h + 2], (span, 2 * SHEAD))

        def two_columns(base, i):
            return jnp.concatenate([columns(base, 2 * i), columns(base, 2 * i + 1)], axis=1)

        following = lax.rem(ctx + 2, 2 * nz)

        def first_copy(j):
            return remote(ending.at[j], s_in.at[j], st_send.at[j], st_recv.at[j], following, tp)

        def state_copy(j):
            return remote(s_out.at[j], s_in.at[j], st_send.at[j], st_recv.at[j], following, tp)

        get_g.wait()
        x_copy(other_rows).wait_recv()
        bt_both = jnp.concatenate([bt_hi, bt_lo], axis=0)

        def find_endings(send):
            for i in range(CHUNKS // 2):
                wide = xg[:, 2 * i * CCOLS : 2 * (i + 1) * CCOLS].astype(F32)
                x_hi, x_lo = split(wide * two_columns(GHEADS, i))
                both = dot(bt_both, x_hi)
                e = both[:STATE] + (both[STATE:] + dot(bt_hi, x_lo))
                for k in range(2):
                    ending[2 * i + k] = e[:, k * CCOLS : (k + 1) * CCOLS]
                    if send:
                        first_copy(2 * i + k).start()

        @pl.when(z == 0)
        def _():
            find_endings(True)

        @pl.when(z > 0)
        def _():
            find_endings(False)

        @pl.when(z == 0)
        def _():
            s_in[...] = jnp.zeros_like(s_in)

        cb = dot3((c_hi, c_lo), (bt_hi, bt_lo)) * inv_col * inv / root
        lower = (
            lax.broadcasted_iota(jnp.int32, (span, span), 0)
            >= lax.broadcasted_iota(jnp.int32, (span, span), 1)
        )
        cb_s[...] = jnp.where(lower, cb, 0.0)

        last = cols[span - 8 : span][7:8]
        skip_row, gain_row = channel_rows(skip_ref, gain_ref, half)

        def pass_state(j):
            state_copy(j).wait_recv()
            h = 2 * j
            fade = lane_pair(
                jnp.exp(last[:, h : h + 1]), jnp.exp(last[:, h + 1 : h + 2]), (1, 2 * SHEAD)
            )
            s_out[j] = s_in[j] * fade + ending[j]
            state_copy(j).start()

        for j in range(CHUNKS):
            h = 2 * j
            xp = xg[:, h * SHEAD : (h + 2) * SHEAD]
            tops = []
            lows = []
            for d in range(2):
                lrow = rows_s[0, h + d : h + d + 1]
                urow = rows_s[1, h + d : h + d + 1]
                lcol = tcols[:, h + d : h + d + 1]
                top = (
                    jnp.exp(jnp.minimum(lcol[:ROWS] - lrow[:, :ROWS], 0.0))
                    * cb_s[:ROWS, :ROWS]
                    * urow[:, :ROWS]
                )
                low = jnp.exp(jnp.minimum(lcol[ROWS:] - lrow, 0.0)) * cb_s[ROWS:] * urow
                tops += split(top)
                lows += split(low)
            top = dot(jnp.concatenate(tops, axis=0), xp[:ROWS])
            low = dot(jnp.concatenate(lows, axis=0), xp)
            lane = lax.broadcasted_iota(jnp.int32, (ROWS, 2 * SHEAD), 1)
            at = slice(h * SHEAD, (h + 2) * SHEAD)
            for first, o in ((0, top), (ROWS, low)):
                local[first : first + ROWS, at] = jnp.where(
                    lane < SHEAD,
                    o[0:ROWS] + o[ROWS : 2 * ROWS],
                    o[2 * ROWS : 3 * ROWS] + o[3 * ROWS : 4 * ROWS],
                )

            if j % 2 == 1:

                @pl.when(jnp.logical_and(z == 1, z < nz - 1))
                def _():
                    pass_state(j - 1)
                    pass_state(j)

                if j > 1:

                    @pl.when(jnp.logical_and(z > 1, z < nz - 1))
                    def _():
                        pass_state(j - 3)
                        pass_state(j - 2)

        block = (
            lax.broadcasted_iota(jnp.int32, (2 * CCOLS, 2 * CCOLS), 0) // SHEAD
            == lax.broadcasted_iota(jnp.int32, (2 * CCOLS, 2 * CCOLS), 1) // SHEAD
        ).astype(F32).astype(BF16)

        def out_copy(i, base):
            at = pl.ds(pl.multiple_of(base * GCOLS + 2 * i * CCOLS, 2 * CCOLS), 2 * CCOLS)
            return remote(
                stage.at[other_rows, pl.ds(2 * i * CCOLS, 2 * CCOLS)],
                out_ref.at[:, at],
                o_send.at[i],
                o_recv.at[i],
                pair,
                tp,
            )

        @pl.when(jnp.logical_and(z > 1, z < nz - 1))
        def _():
            pass_state(CHUNKS - 2)
            pass_state(CHUNKS - 1)

        c_both = c_s[...].reshape(2 * span, STATE)
        for i in range(CHUNKS // 2):

            @pl.when(jnp.logical_and(z > 0, z == nz - 1))
            def _():
                state_copy(2 * i).wait_recv()
                state_copy(2 * i + 1).wait_recv()

            at = slice(2 * i * CCOLS, 2 * (i + 1) * CCOLS)
            xc = xg[:, at].astype(F32)
            s_hi, s_lo = split(jnp.concatenate([s_in[2 * i], s_in[2 * i + 1]], axis=1))
            both = dot(c_both, s_hi)
            inflow = both[:span] + (both[span:] + dot(c_s[0], s_lo))
            mixed = (
                local[:, at]
                + inflow * two_columns(2 * GHEADS, i)
                + skip_row[:, at] * (xc * inv_col)
            )
            p_hi, p_lo = split(mixed * mixed)
            power = (dot(p_hi, block) + dot(p_lo, block)) / SHEAD
            stage[:, at] = (xc + gain_row[:, at] * mixed * lax.rsqrt(power + EPSILON)).astype(BF16)
            out_copy(i, half).start()
            to = pl.ds(pl.multiple_of(half * GCOLS + 2 * i * CCOLS, 2 * CCOLS), 2 * CCOLS)
            out_ref[:, to] = stage[my_rows, at]

        for j in range(CHUNKS):
            if j % 2 == 1:
                out_copy(j // 2, half).wait_send()
                out_copy(j // 2, other).wait_recv()

        @pl.when(z < nz - 1)
        def _():
            for j in range(CHUNKS):
                state_copy(j).wait_send()

        for k in range(3):
            p_copy(k, me4).wait_send()
        x_copy(my_rows).wait_send()


def body(queries, keys, values, layer_in, w_bc, w_dt, dt_bias, decay_rate, skip_gain, out_gain):
    nctx = lax.axis_size("ctx")
    nz = nctx // 2
    span = 2 * ROWS
    hbm_spec = pl.BlockSpec(memory_space=pltpu.HBM)
    vmem_spec = pl.BlockSpec(memory_space=pltpu.VMEM)
    dma = pltpu.SemaphoreType.DMA
    vm = pltpu.VMEM
    out = pl.pallas_call(
        functools.partial(kernel, nz),
        out_shape=pltpu.VMEM(layer_in.shape, BF16),
        in_specs=[hbm_spec] * 6 + [vmem_spec] * 4,
        out_specs=vmem_spec,
        scratch_shapes=[
            vm(queries.shape, BF16),
            vm(keys.shape, BF16),
            vm(values.shape, BF16),
            vm((2, QH, ROWS, HEAD), BF16),
            vm((2, 4, ROWS, HEAD), BF16),
            vm((QH, span, HEAD), BF16),
            vm((nz, 4, span, HEAD), BF16),
            vm((nz, 2 * span, span), F32),
            vm(layer_in.shape, BF16),
            vm(w_bc.shape[1:], BF16),
            vm((w_dt.shape[2], w_dt.shape[1]), BF16),
            vm((span, GCOLS), BF16),
            vm((GROUPS - 1, PACK, STATE), F32),
            vm((GROUPS * GHEADS, ROWS), F32),
            vm((GROUPS, PACK, STATE), F32),
            vm((span, STATE), F32),
            vm((2, GHEADS, span), F32),
            vm((8, STATE), BF16),
            vm((2, span, STATE), BF16),
            vm((span, span), F32),
            vm((CHUNKS, STATE, CCOLS), F32),
            vm((CHUNKS, STATE, CCOLS), F32),
            vm((CHUNKS, STATE, CCOLS), F32),
            vm((span, GCOLS), F32),
            vm((span, GCOLS), BF16),
            dma((4,)),
            dma((2,)),
            dma((2,)),
            dma((2 * nz,)),
            dma((2 * nz,)),
            dma((2,)),
            dma((3,)),
            dma((3,)),
            dma((CHUNKS,)),
            dma((CHUNKS,)),
            dma((CHUNKS,)),
            dma((CHUNKS,)),
        ],
        compiler_params=pltpu.CompilerParams(
            collective_id=0, has_side_effects=True, vmem_limit_bytes=60 * 1024 * 1024
        ),
    )(
        queries,
        keys,
        values,
        layer_in,
        w_bc[0],
        w_dt[0].T,
        dt_bias,
        decay_rate,
        skip_gain,
        out_gain[0],
    )
    return out[None]


def solution(mesh):
    in_specs = (
        P("ctx", "tp", None),
        P("ctx", "tp", None),
        P("ctx", "tp", None),
        P("ctx", "tp"),
        P(None, "tp", None),
        P(None, "tp", None),
        P(None, "tp"),
        P(None, "tp"),
        P(None, "tp"),
        P(None, "tp", None),
    )
    out_specs = P("segment", "ctx", "tp")
    return jax.shard_map(body, mesh=mesh, in_specs=in_specs, out_specs=out_specs, check_vma=False)
```
